256 devices in a mesh: group: 8 (over z_hi, core), tp: 32 (over x, y, z_lo).
Axes of the slice: x: 4, y: 4, z: 8 (z_hi: 4, z_lo: 2; z = z_hi * 2 + z_lo), core: 2. Of those that a mesh axis runs over, the one named last changes fastest.
Arguments:
- prefill_x: bfloat16 [1024, 16384], P('group', 'tp'), may hold values from -6 to 6
- prefill_gate: bfloat16 [1024, 16384], P('group', 'tp'), may hold values from -6 to 6
- lengths: int32 [8, 8], P('group'), may hold values from 1 to 64, 128 in all within a row
- routes: int32 [64, 1], replicated, may hold values from 0 to 7; in each aligned block of 8 rows (0 to 7, 8 to 15, ...) at most 2 rows name the same one
- decode_x: bfloat16 [4, 256, 16384], P(None, 'group', 'tp'), may hold values from -6 to 6
- decode_gate: bfloat16 [4, 256, 16384], P(None, 'group', 'tp'), may hold values from -6 to 6
- cached_state: float32 [256, 16, 16384], P('group', None, 'tp'), may hold values from -4 to 4
- xproj_weight: bfloat16 [16384, 544], P('tp'), may hold values from -0.046875 to 0.046875
- dt_weight: bfloat16 [512, 16384], P(None, 'tp'), may hold values from -0.25 to 0.25
- dt_bias: float32 [16384], P('tp'), may hold values from -3 to -1
- a_log: float32 [16, 16384], P(None, 'tp'), may hold values from 0 to 2.77
- skip_gain: float32 [16384], P('tp'), may hold values from 0.5 to 1.5
Outputs:
- prefill_out: bfloat16 [1024, 16384], P('group', 'tp')
- decode_out: bfloat16 [4, 256, 16384], P(None, 'group', 'tp')
The draws below stay inside these ranges and needn't reach their ends.
Inputs may be any that keep to these rules, and one draw needn't show every extreme that they name: `routes`: in each aligned block of 8 rows (the requests of one group) no decode group is named more than 2 times. `lengths`: each group's row sums to 128; its largest entry is 64.
All inputs are finite; a program needn't handle non-finite values.
Results may differ from the reference program's by a relative error of at most 0.0051.
Values sent between devices are 32-bit elements; how exact they have to be, the bound alone decides.
No kernel may reach another device: no remote copies, remote signals or barrier semaphores. Data moves between devices by JAX's collectives and lax.ppermute only.
A program may use at most 64 MiB of HBM per device.

```python
import math
import jax
import jax.numpy as jnp
import numpy as np
from jax import lax

E = 16384
S = 16
DT_RANK = 512
TOK = 128
REQ = 8
ROWS = 32
STEPS = 4
MAXLEN = 64
CAP = 2
N_GROUP = 8


def level_of(key, extent, pieces, smallest, top_value):
    def one(axis_at, parts):
        heights = jax.random.uniform(jax.random.fold_in(jax.random.fold_in(key, 6), axis_at), (parts,), jnp.float32, smallest / len(pieces), top_value / len(pieces))
        return jnp.repeat(jnp.exp(heights), extent[axis_at] // parts).reshape((-1,) + (1,) * (len(extent) - axis_at - 1))

    level = one(*pieces[0])
    for cut in pieces[1:]:
        level = level * one(*cut)
    return level


def length_profile(count, total, bound, lean):
    loads = [(1 << 20) // math.isqrt(rank ** lean) + 1 for rank in range(2, count + 1)]
    spare, given = total - bound - (count - 1), [1] * (count - 1)
    while spare > 0:
        candidates = [i for i in range(count - 1) if given[i] < bound]
        mass, budget = sum([loads[i] for i in candidates]), spare
        for i in candidates:
            more = min(bound - given[i], max(1, budget * loads[i] // mass), spare)
            given[i] = given[i] + more
            spare = spare - more
    return np.array([bound] + given)


def uneven(stream_key, amount, total, most, slope):
    if amount == 2:
        one = jax.random.randint(stream_key, (), max(1, total - most), min(most, total - 1) + 1)
        return jnp.stack([one, total - one])
    sizes = jnp.asarray(length_profile(amount, total, most, slope), jnp.int32)
    couples = (amount - 1) // 2
    donor, sink = sizes[1:1 + 2 * couples:2], sizes[2:2 + 2 * couples:2]
    margin = jnp.minimum(donor - 1, most - sink)
    moved = jax.random.randint(jax.random.fold_in(stream_key, 1), (couples,), 0, 1 << 20) % (margin + 1)
    sizes = sizes.at[1:1 + 2 * couples:2].set(donor - moved).at[2:2 + 2 * couples:2].set(sink + moved)
    return sizes[jax.random.permutation(jax.random.fold_in(stream_key, 2), amount)]


def assign_block(own_key, own, number, rows, count, top, most, lean):
    ranking = jax.random.permutation(own_key, count)
    heavy_load, ordinary = shares(count, rows * top, most, lean, True), shares(count, rows * top, most, lean, False)
    places = jnp.arange(count)

    def named(tallies, rotation):
        used = int((tallies > 0).sum())
        fixed = max(1, used // 4)
        shifted = fixed + (places - fixed + rotation * (used - fixed)) % max(1, count - fixed)
        return jnp.zeros((count,), jnp.int32).at[ranking[jnp.where(places < fixed, places, shifted)]].set(jnp.asarray(tallies, jnp.int32))

    tallies = jnp.where(number % 4 == 0, named(heavy_load, number // 4), named(ordinary, number - number // 4 - 1))
    mixed = jax.random.permutation(jax.random.fold_in(own, 3), count)
    source_of, taker = mixed[0:count // 2 * 2:2], mixed[1:count // 2 * 2:2]
    margin = jnp.minimum(tallies[source_of] - 1, most - tallies[taker]) // 2
    margin = jnp.where((source_of == ranking[0]) | (taker == ranking[0]) | (tallies[taker] == 0), 0, jnp.maximum(margin, 0))
    shifted = jax.random.randint(jax.random.fold_in(own, 4), (count // 2,), 0, 1 << 20) % (margin + 1)
    tallies = tallies.at[source_of].add(-shifted).at[taker].add(shifted)
    members = jnp.searchsorted(jnp.cumsum(tallies), jnp.arange(rows * top), side="right").astype(jnp.int32)
    table = members.reshape(top, rows).T
    table = table[jax.random.permutation(jax.random.fold_in(own, 1), rows)]
    rotation = jax.random.randint(jax.random.fold_in(own, 2), (rows, 1), 0, top)
    return jnp.take_along_axis(table, (jnp.arange(top)[None, :] + rotation) % top, axis=1)


def shares(count, total, most, lean, full):
    weights = [(1 << 20) // math.isqrt(grade ** lean) + 1 for grade in range(1, count + 1)]
    largest = most if full else min(most, max(-(-total // count), total * weights[0] // sum(weights)))
    least = 1 if total - largest >= count - 1 else 0
    counts, spare = [largest] + [least] * (count - 1), total - largest - least * (count - 1)
    while spare > 0:
        free = [i for i in range(1, count) if counts[i] < largest] or [i for i in range(1, count) if counts[i] < most]
        mass, budget = sum([weights[i] for i in free]), spare
        for i in free:
            extra = min(most - counts[i], max(1, budget * weights[i] // mass), spare)
            counts[i] = counts[i] + extra
            spare = spare - extra
    return np.array(counts)


def scatter_about(own_key, extent, spread, reach, pieces=(), held_as=jnp.bfloat16):
    loudness = level_of(own_key, extent, pieces, -0.22, 0.18) if pieces else 1.0
    drawn = jax.random.normal(own_key, extent, jnp.float32) * spread * loudness
    return jnp.minimum(jnp.maximum(drawn, -reach), reach).astype(held_as)


def setup_inputs(seed: int = 0) -> dict:
    seeds = jax.random.split(jax.random.key(seed), 13)
    prefill_x = scatter_about(seeds[0], (N_GROUP * TOK, E), 1.0, 6.0, ((0, 8), (1, 32)))
    prefill_gate = scatter_about(seeds[1], (N_GROUP * TOK, E), 1.0, 6.0, ((0, 8), (1, 32)))
    lengths = jax.vmap(lambda own: uneven(own, REQ, TOK, MAXLEN, 2))(jax.random.split(seeds[2], N_GROUP)).reshape((N_GROUP, REQ)).astype(jnp.int32)
    routes_keys = jax.random.split(jax.random.fold_in(seeds[3], 1), (N_GROUP * REQ) // REQ)
    routes_turns = jax.random.permutation(jax.random.fold_in(seeds[3], 3), (N_GROUP * REQ) // REQ)
    routes = jax.vmap(lambda own, number: assign_block(jax.random.fold_in(seeds[3], 2), own, number, REQ, N_GROUP, 1, CAP, 2))(routes_keys, routes_turns).reshape((N_GROUP * REQ, 1))
    decode_x = scatter_about(seeds[4], (STEPS, N_GROUP * ROWS, E), 1.0, 6.0, ((1, 8), (2, 32)))
    decode_gate = scatter_about(seeds[5], (STEPS, N_GROUP * ROWS, E), 1.0, 6.0, ((1, 8), (2, 32)))
    cached_state = scatter_about(seeds[6], (N_GROUP * ROWS, S, E), 0.5, 4.0, ((0, 8), (2, 32)), jnp.float32)
    xproj_weight = scatter_about(seeds[7], (E, DT_RANK + 2 * S), E ** -0.5, 0.046875, ((0, 32),))
    dt_weight = scatter_about(seeds[8], (DT_RANK, E), DT_RANK ** -0.5, 0.25, ((1, 32),))
    dt_bias = jnp.clip(-3.0 + 2.0 * jax.random.uniform(seeds[9], (E,), jnp.float32) ** level_of(seeds[9], (E,), ((0, 32),), -0.2, 0.2), -3.0, -1.0)
    a_log = jnp.clip(2.77 * jax.random.uniform(seeds[10], (S, E), jnp.float32) ** level_of(seeds[10], (S, E), ((1, 32),), -0.2, 0.2), 0.0, 2.77)
    skip_gain = jnp.clip(0.5 + 1.0 * jax.random.uniform(seeds[11], (E,), jnp.float32) ** level_of(seeds[11], (E,), ((0, 32),), -0.2, 0.2), 0.5, 1.5)
    return dict(prefill_x=prefill_x, prefill_gate=prefill_gate, lengths=lengths, routes=routes, decode_x=decode_x, decode_gate=decode_gate, cached_state=cached_state, xproj_weight=xproj_weight, dt_weight=dt_weight, dt_bias=dt_bias, a_log=a_log, skip_gain=skip_gain)


def mixer_terms(projected, dt_weight, dt_bias):
    low_part = projected[:, :DT_RANK].astype(jnp.bfloat16)
    step_size = jax.nn.softplus(jnp.dot(low_part, dt_weight, preferred_element_type=jnp.float32) + dt_bias)
    return step_size, projected[:, DT_RANK:DT_RANK + S], projected[:, DT_RANK + S:]


def prefill_group(operands, xproj_weight, dt_weight, dt_bias, rates, skip_gain):
    inputs, gate_rows, lengths_here = operands
    projected = jnp.dot(inputs, xproj_weight, preferred_element_type=jnp.float32)
    step_size, inject, readout = mixer_terms(projected, dt_weight, dt_bias)
    request_end = (jnp.cumsum(lengths_here) - 1).astype(jnp.int32)
    request_start = (request_end - lengths_here + 1).astype(jnp.int32)
    position = jnp.arange(TOK, dtype=jnp.int32)
    first_token = jnp.any(position[:, None] == request_start[None, :], axis=1)
    last_token = jnp.any(position[:, None] == request_end[None, :], axis=1)
    request_of = (jnp.sum((position[:, None] >= request_start[None, :]).astype(jnp.int32), axis=1) - 1).astype(jnp.int32)
    survive = jnp.where(first_token, jnp.float32(0.0), jnp.float32(1.0))
    values = inputs.astype(jnp.float32)

    def advance(carried, slices):
        hidden, final_states = carried
        size_row, inject_row, readout_row, value_row, survive_one, last_one, request_one = slices
        hidden = (survive_one * jnp.exp(size_row[None, :] * rates)) * hidden + (size_row[None, :] * inject_row[:, None]) * value_row[None, :]
        mixed = jnp.sum(readout_row[:, None] * hidden, axis=0)
        previous = lax.dynamic_index_in_dim(final_states, request_one, 0, keepdims=False)
        final_states = lax.dynamic_update_index_in_dim(final_states, jnp.where(last_one, hidden, previous), request_one, 0)
        return (hidden, final_states), mixed

    initial = (jnp.zeros((S, E), jnp.float32), jnp.zeros((REQ, S, E), jnp.float32))
    (hidden, final_states), mixed = lax.scan(advance, initial, (step_size, inject, readout, values, survive, last_token, request_of))
    output = ((mixed + skip_gain * values) * jax.nn.silu(gate_rows.astype(jnp.float32))).astype(jnp.bfloat16)
    return output, final_states


def decode_group(operands, xproj_weight, dt_weight, dt_bias, rates, skip_gain):
    hidden, inputs_all, gates_all = operands
    outputs = []
    for step_index in range(STEPS):
        inputs = inputs_all[step_index]
        projected = jnp.dot(inputs, xproj_weight, preferred_element_type=jnp.float32)
        step_size, inject, readout = mixer_terms(projected, dt_weight, dt_bias)
        values = inputs.astype(jnp.float32)
        hidden = jnp.exp(step_size[:, None, :] * rates[None]) * hidden + (step_size[:, None, :] * inject[:, :, None]) * values[:, None, :]
        mixed = jnp.sum(readout[:, :, None] * hidden, axis=1)
        gate_rows = gates_all[step_index].astype(jnp.float32)
        outputs.append(((mixed + skip_gain * values) * jax.nn.silu(gate_rows)).astype(jnp.bfloat16))
    return jnp.stack(outputs)


def reference(prefill_x, prefill_gate, lengths, routes, decode_x, decode_gate, cached_state, xproj_weight, dt_weight, dt_bias, a_log, skip_gain):
    rates = -jnp.exp(a_log)
    prefill_out, final_states = lax.map(
        lambda operands: prefill_group(operands, xproj_weight, dt_weight, dt_bias, rates, skip_gain),
        (prefill_x.reshape(N_GROUP, TOK, E), prefill_gate.reshape(N_GROUP, TOK, E), lengths))
    prefill_out = prefill_out.reshape(N_GROUP * TOK, E)
    final_states = final_states.reshape(N_GROUP * REQ, S, E)
    flat_routes = routes[:, 0]
    ordering = jnp.arange(N_GROUP * REQ, dtype=jnp.int32)
    same_dest = flat_routes[:, None] == flat_routes[None, :]
    slot_index = jnp.sum(((ordering[:, None] > ordering[None, :]) & same_dest).astype(jnp.int32), axis=1).astype(jnp.int32)
    targets = (flat_routes * ROWS + slot_index).astype(jnp.int32)
    row_ids = jnp.arange(N_GROUP * ROWS, dtype=jnp.int32)
    matches = row_ids[:, None] == targets[None, :]
    arrived = jnp.any(matches, axis=1)
    source = jnp.argmax(matches.astype(jnp.int32), axis=1).astype(jnp.int32)
    start_state = jnp.where(arrived[:, None, None], final_states[source], cached_state)
    decode_out = lax.map(
        lambda operands: decode_group(operands, xproj_weight, dt_weight, dt_bias, rates, skip_gain),
        (start_state.reshape(N_GROUP, ROWS, S, E),
         decode_x.reshape(STEPS, N_GROUP, ROWS, E).transpose(1, 0, 2, 3),
         decode_gate.reshape(STEPS, N_GROUP, ROWS, E).transpose(1, 0, 2, 3)))
    decode_out = decode_out.transpose(1, 0, 2, 3).reshape(STEPS, N_GROUP * ROWS, E)
    return prefill_out, decode_out
```

```python
import functools

import jax
import jax.numpy as jnp
from jax import lax
from jax.experimental import pallas as pl
from jax.experimental.pallas import tpu as pltpu
from jax.sharding import PartitionSpec as P

LOG2E = 1.4426950408889634
FAR = 1e30
LANES = 128
VMEM_LIMIT = 40 * 1024 * 1024

VMEM = pl.BlockSpec(memory_space=pltpu.VMEM)
SMEM = pl.BlockSpec(memory_space=pltpu.SMEM)


def params():
    return pltpu.CompilerParams(vmem_limit_bytes=VMEM_LIMIT)


def softplus(v):
    return jnp.maximum(v, 0.0) + jnp.log1p(jnp.exp(-jnp.abs(v)))


def silu(v):
    return v / (1.0 + jnp.exp(-v))


def project_kernel(prefill_ref, decode_ref, weight_ref, out_ref):
    tokens = prefill_ref.shape[0]
    weight = weight_ref[...]
    half = out_ref.shape[0] // 2
    first = jnp.dot(prefill_ref[...], weight, preferred_element_type=jnp.float32)
    out_ref[:half] = first.reshape(half, tokens // half, -1)
    second = jnp.dot(decode_ref[...], weight, preferred_element_type=jnp.float32)
    out_ref[half:] = second.reshape(half, tokens // half, -1)


def total_kernel(parts_ref, out_ref):
    total = jnp.sum(parts_ref[...], axis=0)
    out_ref[...] = jnp.broadcast_to(total[None], out_ref.shape)


def step_sizes(proj, weight_ref, bias_ref):
    rank = weight_ref.shape[0]
    low = proj[:, :rank].astype(jnp.bfloat16)
    return softplus(
        jnp.dot(low, weight_ref[...], preferred_element_type=jnp.float32) + bias_ref[...]
    )


def advance(hidden, rates_ref, size_row, forcing_row, inject, readout):
    mixed = []
    for tile in range(len(hidden)):
        cols = slice(tile * LANES, (tile + 1) * LANES)
        damping = jnp.exp2(size_row[:, cols] * rates_ref[:, cols])
        hidden[tile] = damping * hidden[tile] + forcing_row[:, cols] * inject
        mixed.append(jnp.sum(readout * hidden[tile], axis=0, keepdims=True))
    return jnp.concatenate(mixed, axis=1)


def prefill_kernel(
    lengths_ref, routes_ref, proj_ref, x_ref, gate_ref, weight_ref, bias_ref, alog_ref, skip_ref,
    out_ref, send_ref,
    size_ref, force_ref, mixed_ref, vec_ref, rates_ref, hist_ref,
):
    tokens, channels = x_ref.shape
    width = alog_ref.shape[0]
    requests = lengths_ref.shape[1]
    rank = weight_ref.shape[0]
    group = lax.axis_index("group")
    proj = proj_ref[...].reshape(tokens, -1)
    size = step_sizes(proj, weight_ref, bias_ref)
    values = x_ref[...].astype(jnp.float32)
    force_ref[...] = size * values
    position = lax.broadcasted_iota(jnp.int32, (tokens, LANES), 0)
    first = position == 0
    begin = jnp.int32(0)
    ends = []
    for k in range(requests):
        first = first | (position == begin)
        begin = begin + lengths_ref[0, k]
        ends.append(begin - 1)
    reset = jnp.where(first, jnp.float32(FAR), jnp.float32(0.0))
    for tile in range(channels // LANES):
        cols = slice(tile * LANES, (tile + 1) * LANES)
        size_ref[:, cols] = size[:, cols] + reset
    vec_ref[...] = jnp.transpose(proj[:, rank:])
    rates_ref[...] = -LOG2E * jnp.exp(alog_ref[...])

    def block(b, hidden):
        base = pl.multiple_of(b * 8, 8)
        vectors = pltpu.roll(vec_ref[...], tokens - base, axis=1)
        sizes = size_ref[pl.ds(base, 8), :]
        forces = force_ref[pl.ds(base, 8), :]
        hidden = list(hidden)
        rows = []
        for i in range(8):
            inject = jnp.broadcast_to(vectors[:width, i : i + 1], (width, LANES))
            readout = jnp.broadcast_to(vectors[width:, i : i + 1], (width, LANES))
            rows.append(
                advance(
                    hidden, rates_ref, sizes[i : i + 1], forces[i : i + 1], inject, readout
                )
            )
            for tile in range(len(hidden)):
                hist_ref[base + i, :, tile * LANES : (tile + 1) * LANES] = hidden[tile]
        mixed_ref[pl.ds(base, 8), :] = jnp.concatenate(rows, axis=0)
        return tuple(hidden)

    zero = jnp.zeros((width, LANES), jnp.float32)
    lax.fori_loop(0, tokens // 8, block, (zero,) * (channels // LANES))
    out_ref[...] = (
        (mixed_ref[...] + skip_ref[...] * values) * silu(gate_ref[...].astype(jnp.float32))
    ).astype(out_ref.dtype)
    dests = [routes_ref[group * requests + k, 0] for k in range(requests)]
    for k in range(requests):
        lane = jnp.int32(0)
        for j in range(k):
            lane = lane + (dests[j] == dests[k]).astype(jnp.int32)
        send_ref[dests[k], lane] = hist_ref[ends[k]]


def decode_kernel(
    routes_ref, proj_ref, recv_ref, state_ref, x_ref, gate_ref, weight_ref, bias_ref, alog_ref,
    skip_ref,
    out_ref,
    size_ref, force_ref, mixed_ref, vec_ref, rates_ref, start_ref,
):
    total, channels = x_ref.shape
    rows, width = state_ref.shape[:2]
    steps = total // rows
    groups, cap = recv_ref.shape[:2]
    requests = routes_ref.shape[0] // groups
    rank = weight_ref.shape[0]
    me = lax.axis_index("group")
    proj = proj_ref[...].reshape(total, -1)
    size = step_sizes(proj, weight_ref, bias_ref)
    values = x_ref[...].astype(jnp.float32)
    size_ref[...] = size
    force_ref[...] = size * values
    vec_ref[...] = jnp.transpose(proj[:, rank:])
    rates_ref[...] = -LOG2E * jnp.exp(alog_ref[...])
    start_ref[...] = state_ref[...]
    slot = jnp.int32(0)
    for g in range(groups):
        count = jnp.int32(0)
        for k in range(requests):
            count = count + (routes_ref[g * requests + k, 0] == me).astype(jnp.int32)
        for c in range(cap):

            @pl.when(count > c)
            def _(g=g, c=c, slot=slot):
                start_ref[slot + c] = recv_ref[g, c]

        slot = slot + count

    def block(b, carry):
        base = pl.multiple_of(b * 8, 8)
        vectors, sizes, forces = [], [], []
        for s in range(steps):
            at = pl.multiple_of(s * rows + base, 8)
            vectors.append(pltpu.roll(vec_ref[...], total - at, axis=1))
            sizes.append(size_ref[pl.ds(at, 8), :])
            forces.append(force_ref[pl.ds(at, 8), :])
        results = [[] for _ in range(steps)]
        for i in range(8):
            hidden = [
                start_ref[base + i, :, tile * LANES : (tile + 1) * LANES]
                for tile in range(channels // LANES)
            ]
            for s in range(steps):
                inject = jnp.broadcast_to(vectors[s][:width, i : i + 1], (width, LANES))
                readout = jnp.broadcast_to(vectors[s][width:, i : i + 1], (width, LANES))
                results[s].append(
                    advance(
                        hidden, rates_ref, sizes[s][i : i + 1], forces[s][i : i + 1], inject, readout
                    )
                )
        for s in range(steps):
            at = pl.multiple_of(s * rows + base, 8)
            mixed_ref[pl.ds(at, 8), :] = jnp.concatenate(results[s], axis=0)
        return carry

    lax.fori_loop(0, rows // 8, block, 0)
    out_ref[...] = (
        (mixed_ref[...] + skip_ref[...] * values) * silu(gate_ref[...].astype(jnp.float32))
    ).astype(out_ref.dtype)


def local(
    prefill_x, prefill_gate, lengths, routes, decode_x, decode_gate, cached_state, xproj_weight,
    dt_weight, dt_bias, a_log, skip_gain, *, ranks, groups, cap,
):
    tokens, channels = prefill_x.shape
    steps, rows, _ = decode_x.shape
    width = a_log.shape[0]
    columns = xproj_weight.shape[1]
    decode_rows = steps * rows
    decode_flat = decode_x.reshape(decode_rows, channels)
    gate_flat = decode_gate.reshape(decode_rows, channels)
    bias = dt_bias.reshape(1, channels)
    skip = skip_gain.reshape(1, channels)
    per = (tokens + decode_rows) // ranks
    chunked = jax.ShapeDtypeStruct((ranks, per, columns), jnp.float32)

    partial = pl.pallas_call(
        project_kernel, out_shape=chunked, in_specs=[VMEM] * 3, out_specs=VMEM,
        compiler_params=params(), name="project",
    )(prefill_x, decode_flat, xproj_weight)
    parts = lax.all_to_all(partial, "tp", 0, 0)
    copies = pl.pallas_call(
        total_kernel, out_shape=chunked, in_specs=[VMEM], out_specs=VMEM,
        compiler_params=params(), name="total",
    )(parts)
    proj = lax.all_to_all(copies, "tp", 0, 0)

    def part(index):
        return pl.BlockSpec((ranks // 2, per, columns), lambda i: (index, 0, 0))

    def f32(*shape):
        return pltpu.VMEM(shape, jnp.float32)

    prefill_out, send = pl.pallas_call(
        prefill_kernel,
        grid=(1,),
        out_shape=(
            jax.ShapeDtypeStruct((tokens, channels), jnp.bfloat16),
            jax.ShapeDtypeStruct((groups, cap, width, channels), jnp.float32),
        ),
        in_specs=[SMEM, SMEM, part(0)] + [VMEM] * 6,
        out_specs=(VMEM, VMEM),
        scratch_shapes=[
            f32(tokens, channels), f32(tokens, channels), f32(tokens, channels),
            f32(2 * width, tokens), f32(width, channels), f32(tokens, width, channels),
        ],
        compiler_params=params(), name="prefill",
    )(lengths, routes, proj, prefill_x, prefill_gate, dt_weight, bias, a_log, skip)
    recv = lax.all_to_all(send, "group", 0, 0)
    decode_out = pl.pallas_call(
        decode_kernel,
        grid=(1,),
        out_shape=jax.ShapeDtypeStruct((decode_rows, channels), jnp.bfloat16),
        in_specs=[SMEM, part(1)] + [VMEM] * 8,
        out_specs=VMEM,
        scratch_shapes=[
            f32(decode_rows, channels), f32(decode_rows, channels), f32(decode_rows, channels),
            f32(2 * width, decode_rows), f32(width, channels), f32(rows, width, channels),
        ],
        compiler_params=params(), name="decode",
    )(routes, proj, recv, cached_state, decode_flat, gate_flat, dt_weight, bias, a_log, skip)
    return prefill_out, decode_out.reshape(steps, rows, channels)


def solution(mesh):
    placed = (
        P("group", "tp"), P("group", "tp"), P("group", None), P(), P(None, "group", "tp"),
        P(None, "group", "tp"), P("group", None, "tp"), P("tp", None), P(None, "tp"), P("tp"),
        P(None, "tp"), P("tp"),
    )
    body = functools.partial(local, ranks=mesh.shape["tp"], groups=mesh.shape["group"], cap=2)
    return jax.shard_map(
        body, mesh=mesh, in_specs=placed, out_specs=(P("group", "tp"), P(None, "group", "tp")),
        check_vma=False,
    )
```

```python
import functools

import jax
import jax.numpy as jnp
from jax import lax
from jax.experimental import pallas as pl
from jax.experimental.pallas import tpu as pltpu
from jax.sharding import PartitionSpec as P

LOG2E = 1.4426950408889634
FAR = 1e30
LANES = 128
CAP = 2

VMEM = pl.BlockSpec(memory_space=pltpu.VMEM)
SMEM = pl.BlockSpec(memory_space=pltpu.SMEM)
ANY = pl.BlockSpec(memory_space=pl.ANY)


def call(kernel, name, out_shape, in_specs, out_specs=VMEM, scratch=(), mib=16, flops=0):
    return pl.pallas_call(
        kernel,
        grid=(1,),
        out_shape=out_shape,
        in_specs=in_specs,
        out_specs=out_specs,
        scratch_shapes=scratch,
        compiler_params=pltpu.CompilerParams(vmem_limit_bytes=mib << 20),
        cost_estimate=pl.CostEstimate(flops=flops, bytes_accessed=1 << 20, transcendentals=0),
        name=name,
    )


def f32(*shape):
    return pltpu.VMEM(shape, jnp.float32)


def bf16(*shape):
    return pltpu.VMEM(shape, jnp.bfloat16)


def struct(shape, dtype=jnp.float32):
    return jax.ShapeDtypeStruct(shape, dtype)


def stay(*arrays):
    return tuple(pltpu.with_memory_space_constraint(a, pltpu.HBM) for a in arrays)


def fetch(sources, targets, sems):
    copies = [
        pltpu.make_async_copy(a, b, sems.at[i]) for i, (a, b) in enumerate(zip(sources, targets))
    ]
    for copy in copies:
        copy.start()
    return copies


def softplus(v):
    return jnp.maximum(v, 0.0) + jnp.log1p(jnp.exp(-jnp.abs(v)))


def silu(v):
    return v / (1.0 + jnp.exp(-v))


def tiles_of(channels):
    return [slice(t, t + LANES) for t in range(0, channels, LANES)]


def project_kernel(
    weight_hbm, prefill_hbm, decode_hbm, out_ref, weight_ref, prefill_ref, decode_ref, sems
):
    copies = fetch(
        (weight_hbm, prefill_hbm, decode_hbm), (weight_ref, prefill_ref, decode_ref), sems
    )
    half = out_ref.shape[0] // 2
    copies[0].wait()
    weight = weight_ref[...]
    for part, ref in enumerate((prefill_ref, decode_ref)):
        copies[part + 1].wait()
        rows = lax.dot_general(
            ref[...], weight, (((1,), (1,)), ((), ())), preferred_element_type=jnp.float32
        )
        out_ref[part * half : (part + 1) * half] = rows.reshape(half, ref.shape[0] // half, -1)


def total_kernel(parts_ref, out_ref):
    total = jnp.sum(parts_ref[...], axis=0)
    out_ref[...] = jnp.broadcast_to(total[None], out_ref.shape)


def step_sizes(proj, weight_ref, bias_ref):
    rank = weight_ref.shape[0]
    low = proj[:, :rank].astype(jnp.bfloat16)
    return softplus(
        jnp.dot(low, weight_ref[...], preferred_element_type=jnp.float32) + bias_ref[...]
    )


def advance(hidden, rates_ref, size_row, forcing_row, inject, readout):
    mixed = []
    for tile, cols in enumerate(tiles_of(size_row.shape[1])):
        damping = jnp.exp2(size_row[:, cols] * rates_ref[:, cols])
        hidden[tile] = damping * hidden[tile] + forcing_row[:, cols] * inject
        if readout is not None:
            mixed.append(jnp.sum(readout * hidden[tile], axis=0, keepdims=True))
    return jnp.concatenate(mixed, axis=1) if mixed else None


def prepare_scan(lengths_ref, proj, x_ref, weight_ref, bias_ref, alog_ref, size_ref, force_ref, vec_ref, rates_ref):
    tokens, channels = x_ref.shape
    size = step_sizes(proj, weight_ref, bias_ref)
    force_ref[...] = size * x_ref[...].astype(jnp.float32)
    position = lax.broadcasted_iota(jnp.int32, (tokens, LANES), 0)
    first = position == 0
    begin = jnp.int32(0)
    ends = []
    for k in range(lengths_ref.shape[1]):
        first = first | (position == begin)
        begin = begin + lengths_ref[0, k]
        ends.append(begin - 1)
    reset = jnp.where(first, jnp.float32(FAR), jnp.float32(0.0))
    for cols in tiles_of(channels):
        size_ref[:, cols] = size[:, cols] + reset
    vec_ref[...] = jnp.transpose(proj[:, weight_ref.shape[0] :])
    rates_ref[...] = -LOG2E * jnp.exp(alog_ref[...])
    return ends


def scan(size_ref, force_ref, vec_ref, rates_ref, mixed_ref, hist_ref):
    tokens, channels = size_ref.shape
    width = rates_ref.shape[0]
    tiles = tiles_of(channels)

    def block(b, hidden):
        base = pl.multiple_of(b * 8, 8)
        vectors = pltpu.roll(vec_ref[...], tokens - base, axis=1)
        sizes = size_ref[pl.ds(base, 8), :]
        forces = force_ref[pl.ds(base, 8), :]
        hidden = list(hidden)
        rows = []
        for i in range(8):
            inject = jnp.broadcast_to(vectors[:width, i : i + 1], (width, LANES))
            readout = None
            if mixed_ref is not None:
                readout = jnp.broadcast_to(vectors[width:, i : i + 1], (width, LANES))
            rows.append(
                advance(hidden, rates_ref, sizes[i : i + 1], forces[i : i + 1], inject, readout)
            )
            if hist_ref is not None:
                for tile, cols in enumerate(tiles):
                    hist_ref[base + i, :, cols] = hidden[tile]
        if mixed_ref is not None:
            mixed_ref[pl.ds(base, 8), :] = jnp.concatenate(rows, axis=0)
        return tuple(hidden)

    zero = jnp.zeros((width, LANES), jnp.float32)
    lax.fori_loop(0, tokens // 8, block, (zero,) * len(tiles))


def states_kernel(
    lengths_ref, routes_ref, proj_ref, x_ref, weight_ref, bias_ref, alog_ref,
    send_ref, size_ref, force_ref, vec_ref, rates_ref, hist_ref, sems,
):
    requests = lengths_ref.shape[1]
    group = lax.axis_index("group")
    proj = proj_ref[...].reshape(x_ref.shape[0], -1)
    ends = prepare_scan(
        lengths_ref, proj, x_ref, weight_ref, bias_ref, alog_ref, size_ref, force_ref, vec_ref,
        rates_ref,
    )
    scan(size_ref, force_ref, vec_ref, rates_ref, None, hist_ref)
    dests = [routes_ref[group * requests + k, 0] for k in range(requests)]
    copies = []
    for k in range(requests):
        lane = jnp.int32(0)
        for j in range(k):
            lane = lane + (dests[j] == dests[k]).astype(jnp.int32)
        copies.append(
            pltpu.make_async_copy(hist_ref.at[ends[k]], send_ref.at[dests[k], lane], sems.at[k])
        )
        copies[-1].start()
    for copy in copies:
        copy.wait()


def rest_kernel(
    lengths_ref, routes_ref, proj_ref,
    state_hbm, decode_x_hbm, decode_gate_hbm, weight_hbm, alog_hbm, bias_hbm, skip_hbm,
    prefill_x_hbm, prefill_gate_hbm,
    out_ref, mixed_ref, unit_ref, source_ref,
    state_ref, decode_x_ref, decode_gate_ref, weight_ref, alog_ref, bias_ref, skip_ref,
    prefill_x_ref, prefill_gate_ref,
    size_ref, force_ref, act_ref, sum_ref, vec_ref, rates_ref, sems, *, groups,
):
    copies = fetch(
        (
            weight_hbm, alog_hbm, bias_hbm, skip_hbm, decode_x_hbm, decode_gate_hbm, state_hbm,
            prefill_x_hbm, prefill_gate_hbm,
        ),
        (
            weight_ref, alog_ref, bias_ref, skip_ref, decode_x_ref, decode_gate_ref, state_ref,
            prefill_x_ref, prefill_gate_ref,
        ),
        sems,
    )
    total, channels = decode_x_ref.shape
    rows, width = state_ref.shape[:2]
    steps = total // rows
    reach = unit_ref.shape[0]
    half = proj_ref.shape[0] // 2
    tiles = tiles_of(channels)
    rank = weight_ref.shape[0]
    requests = lengths_ref.shape[1]
    me = lax.axis_index("group")
    for n in range(reach):
        source_ref[n] = -1
    slot = jnp.int32(0)
    for g in range(groups):
        lane = jnp.int32(0)
        for k in range(requests):
            ours = routes_ref[g * requests + k, 0] == me

            @pl.when(ours)
            def _(g=g, slot=slot, lane=lane):
                source_ref[slot] = g * CAP + lane

            slot = slot + ours.astype(jnp.int32)
            lane = lane + ours.astype(jnp.int32)

    for copy in copies[:5]:
        copy.wait()
    proj = proj_ref[half:].reshape(total, -1)
    size = step_sizes(proj, weight_ref, bias_ref)
    values = decode_x_ref[...].astype(jnp.float32)
    size_ref[...] = size
    force_ref[...] = size * values
    vec_ref[...] = jnp.transpose(proj[:, rank:])
    rates_ref[...] = -LOG2E * jnp.exp(alog_ref[...])
    copies[5].wait()
    act_ref[...] = silu(decode_gate_ref[...].astype(jnp.float32))
    copies[6].wait()

    def block(b, carry, units):
        base = pl.multiple_of(b * 8, 8)
        at = [pl.multiple_of(s * rows + base, 8) for s in range(steps)]
        vectors = [pltpu.roll(vec_ref[...], total - at[s], axis=1) for s in range(steps)]
        sizes = [size_ref[pl.ds(at[s], 8), :] for s in range(steps)]
        forces = [force_ref[pl.ds(at[s], 8), :] for s in range(steps)]
        acts = [act_ref[pl.ds(at[s], 8), :] for s in range(steps)]
        results = [[] for _ in range(steps)]
        for i in range(8):
            hidden = [state_ref[base + i, :, cols] for cols in tiles]
            if units:
                taken = source_ref[base + i] >= 0
                hidden = [jnp.where(taken, 0.0, start) for start in hidden]
            summed = None
            for s in range(steps):
                inject = jnp.broadcast_to(vectors[s][:width, i : i + 1], (width, LANES))
                readout = jnp.broadcast_to(vectors[s][width:, i : i + 1], (width, LANES))
                row = sizes[s][i : i + 1]
                results[s].append(
                    advance(hidden, rates_ref, row, forces[s][i : i + 1], inject, readout)
                )
                if units:
                    summed = row if s == 0 else summed + row
                    for cols in tiles:
                        unit_ref[base + i, s, :, cols] = (
                            readout * acts[s][i : i + 1, cols]
                        ) * jnp.exp2(summed[:, cols] * rates_ref[:, cols])
        for s in range(steps):
            sum_ref[pl.ds(at[s], 8), :] = jnp.concatenate(results[s], axis=0)
        return carry

    lax.fori_loop(0, reach // 8, functools.partial(block, units=True), 0)
    lax.fori_loop(reach // 8, rows // 8, functools.partial(block, units=False), 0)
    mixed_ref[...] = (sum_ref[...] + skip_ref[...] * values) * act_ref[...]

    copies[7].wait()
    proj = proj_ref[:half].reshape(total, -1)
    prepare_scan(
        lengths_ref, proj, prefill_x_ref, weight_ref, bias_ref, alog_ref, size_ref, force_ref,
        vec_ref, rates_ref,
    )
    scan(size_ref, force_ref, vec_ref, rates_ref, sum_ref, None)
    copies[8].wait()
    mixed = sum_ref[...] + skip_ref[...] * prefill_x_ref[...].astype(jnp.float32)
    out_ref[...] = (mixed * silu(prefill_gate_ref[...].astype(jnp.float32))).astype(out_ref.dtype)


def combine_kernel(source_ref, mixed_ref, unit_ref, recv_ref, out_ref):
    reach, steps = unit_ref.shape[:2]
    rows = mixed_ref.shape[0] // steps
    added = [[] for _ in range(steps)]
    for n in range(reach):
        source = source_ref[n]
        state = jnp.where(source >= 0, recv_ref[jnp.maximum(source, 0)], 0.0)
        for s in range(steps):
            added[s].append(jnp.sum(unit_ref[n, s] * state, axis=0, keepdims=True))
    for s in range(steps):
        first, last = s * rows, (s + 1) * rows
        out_ref[first : first + reach, :] = (
            mixed_ref[first : first + reach, :] + jnp.concatenate(added[s], axis=0)
        ).astype(out_ref.dtype)
        out_ref[first + reach : last, :] = mixed_ref[first + reach : last, :].astype(out_ref.dtype)


def local(
    prefill_x, prefill_gate, lengths, routes, decode_x, decode_gate, cached_state, xproj_weight,
    dt_weight, dt_bias, a_log, skip_gain, *, ranks, groups,
):
    tokens, channels = prefill_x.shape
    steps, rows, _ = decode_x.shape
    width = a_log.shape[0]
    requests = lengths.shape[1]
    columns = xproj_weight.shape[1]
    total = steps * rows
    reach = groups * CAP
    decode_flat = decode_x.reshape(total, channels)
    gate_flat = decode_gate.reshape(total, channels)
    bias = dt_bias.reshape(1, channels)
    skip = skip_gain.reshape(1, channels)
    per = (tokens + total) // ranks
    chunked = struct((ranks, per, columns))

    partial = call(
        project_kernel, "project", chunked, [ANY] * 3,
        scratch=[
            bf16(columns, channels), bf16(tokens, channels), bf16(total, channels),
            pltpu.SemaphoreType.DMA((3,)),
        ],
    )(*stay(xproj_weight.T, prefill_x, decode_flat))
    parts = lax.all_to_all(partial, "tp", 0, 0)
    copies = call(total_kernel, "total", chunked, [VMEM])(parts)
    proj = lax.all_to_all(copies, "tp", 0, 0)

    scan_scratch = [
        f32(tokens, channels), f32(tokens, channels), f32(2 * width, tokens), f32(width, channels)
    ]
    send = call(
        states_kernel, "states", struct((groups, CAP, width, channels)),
        [SMEM, SMEM, pl.BlockSpec((ranks // 2, per, columns), lambda i: (0, 0, 0))] + [VMEM] * 4,
        out_specs=ANY,
        scratch=scan_scratch
        + [f32(tokens, width, channels), pltpu.SemaphoreType.DMA((requests,))],
    )(lengths, routes, proj, prefill_x, dt_weight, bias, a_log)
    recv = lax.all_to_all(send, "group", 0, 0)
    prefill_out, mixed, unit, source = call(
        functools.partial(rest_kernel, groups=groups), "rest",
        (
            struct((tokens, channels), jnp.bfloat16), struct((total, channels)),
            struct((reach, steps, width, channels)), struct((reach,), jnp.int32),
        ),
        [SMEM, SMEM, VMEM] + [ANY] * 9,
        out_specs=(VMEM, VMEM, VMEM, SMEM),
        scratch=[
            f32(rows, width, channels), bf16(total, channels), bf16(total, channels),
            bf16(*dt_weight.shape), f32(width, channels), f32(1, channels), f32(1, channels),
            bf16(tokens, channels), bf16(tokens, channels),
            f32(total, channels), f32(total, channels), f32(total, channels),
            f32(total, channels), f32(2 * width, total), f32(width, channels),
            pltpu.SemaphoreType.DMA((9,)),
        ],
        flops=8 * 10**9,
    )(
        lengths, routes, proj,
        *stay(
            cached_state, decode_flat, gate_flat, dt_weight, a_log, bias, skip, prefill_x,
            prefill_gate,
        ),
    )
    decode_out = call(
        combine_kernel, "combine", struct((total, channels), jnp.bfloat16), [SMEM] + [VMEM] * 3
    )(source, mixed, unit, recv.reshape(reach, width, channels))
    return prefill_out, decode_out.reshape(steps, rows, channels)


def solution(mesh):
    placed = (
        P("group", "tp"), P("group", "tp"), P("group", None), P(), P(None, "group", "tp"),
        P(None, "group", "tp"), P("group", None, "tp"), P("tp", None), P(None, "tp"), P("tp"),
        P(None, "tp"), P("tp"),
    )
    body = functools.partial(local, ranks=mesh.shape["tp"], groups=mesh.shape["group"])
    return jax.shard_map(
        body, mesh=mesh, in_specs=placed, out_specs=(P("group", "tp"), P(None, "group", "tp")),
        check_vma=False,
    )
```

```python
import functools

import jax
import jax.numpy as jnp
from jax import lax
from jax.experimental import pallas as pl
from jax.experimental.pallas import tpu as pltpu
from jax.sharding import PartitionSpec as P

LOG2E = 1.4426950408889634
FAR = 1e30
LANES = 128
CAP = 2

VMEM = pl.BlockSpec(memory_space=pltpu.VMEM)
SMEM = pl.BlockSpec(memory_space=pltpu.SMEM)
ANY = pl.BlockSpec(memory_space=pl.ANY)


def call(kernel, name, out_shape, in_specs, out_specs=VMEM, scratch=(), mib=16, flops=0):
    return pl.pallas_call(
        kernel,
        grid=(1,),
        out_shape=out_shape,
        in_specs=in_specs,
        out_specs=out_specs,
        scratch_shapes=scratch,
        compiler_params=pltpu.CompilerParams(vmem_limit_bytes=mib << 20),
        cost_estimate=pl.CostEstimate(flops=flops, bytes_accessed=1 << 20, transcendentals=0),
        name=name,
    )


def f32(*shape):
    return pltpu.VMEM(shape, jnp.float32)


def bf16(*shape):
    return pltpu.VMEM(shape, jnp.bfloat16)


def struct(shape, dtype=jnp.float32):
    return jax.ShapeDtypeStruct(shape, dtype)


def stay(*arrays):
    return tuple(pltpu.with_memory_space_constraint(a, pltpu.HBM) for a in arrays)


def fetch(sources, targets, sems):
    copies = [
        pltpu.make_async_copy(a, b, sems.at[i]) for i, (a, b) in enumerate(zip(sources, targets))
    ]
    for copy in copies:
        copy.start()
    return copies


def softplus(v):
    return jnp.maximum(v, 0.0) + jnp.log1p(jnp.exp(-jnp.abs(v)))


def silu(v):
    return v / (1.0 + jnp.exp(-v))


def tiles_of(channels):
    return [slice(t, t + LANES) for t in range(0, channels, LANES)]


def project_kernel(
    weight_hbm, prefill_hbm, decode_hbm, out_ref, weight_ref, prefill_ref, decode_ref, sems
):
    copies = fetch(
        (weight_hbm, prefill_hbm, decode_hbm), (weight_ref, prefill_ref, decode_ref), sems
    )
    half = out_ref.shape[0] // 2
    copies[0].wait()
    weight = weight_ref[...]
    for part, ref in enumerate((prefill_ref, decode_ref)):
        copies[part + 1].wait()
        rows = lax.dot_general(
            ref[...], weight, (((1,), (1,)), ((), ())), preferred_element_type=jnp.float32
        )
        out_ref[part * half : (part + 1) * half] = rows.reshape(half, ref.shape[0] // half, -1)


def total_kernel(parts_ref, out_ref):
    total = jnp.sum(parts_ref[...], axis=0)
    out_ref[...] = jnp.broadcast_to(total[None], out_ref.shape)


def step_sizes(proj, weight_ref, bias_ref):
    rank = weight_ref.shape[0]
    low = proj[:, :rank].astype(jnp.bfloat16)
    return softplus(
        jnp.dot(low, weight_ref[...], preferred_element_type=jnp.float32) + bias_ref[...]
    )


def fold(terms):
    return sum(terms[i : i + 8] for i in range(8, terms.shape[0], 8)) + terms[:8]


def gather_sums(part_ref, first, stride):
    return jnp.concatenate(
        [
            sum(
                (part_ref[tile, pl.ds(first + j, 8, stride=stride), :] for j in range(1, 8)),
                part_ref[tile, pl.ds(first, 8, stride=stride), :],
            )
            for tile in range(part_ref.shape[0])
        ],
        axis=1,
    )


def advance(hidden, rates_ref, size_row, forcing_row, inject, readout, part_ref, at):
    for tile, cols in enumerate(tiles_of(size_row.shape[1])):
        damping = jnp.exp2(size_row[:, cols] * rates_ref[:, cols])
        hidden[tile] = damping * hidden[tile] + forcing_row[:, cols] * inject
        if readout is not None:
            part_ref[tile, at : at + 8, :] = fold(readout * hidden[tile])


def prepare_scan(lengths_ref, proj, x_ref, weight_ref, bias_ref, alog_ref, size_ref, force_ref, vec_ref, rates_ref):
    tokens, channels = x_ref.shape
    size = step_sizes(proj, weight_ref, bias_ref)
    force_ref[...] = size * x_ref[...].astype(jnp.float32)
    position = lax.broadcasted_iota(jnp.int32, (tokens, LANES), 0)
    first = position == 0
    begin = jnp.int32(0)
    ends = []
    for k in range(lengths_ref.shape[1]):
        first = first | (position == begin)
        begin = begin + lengths_ref[0, k]
        ends.append(begin - 1)
    reset = jnp.where(first, jnp.float32(FAR), jnp.float32(0.0))
    for cols in tiles_of(channels):
        size_ref[:, cols] = size[:, cols] + reset
    vec_ref[...] = jnp.transpose(proj[:, weight_ref.shape[0] :])
    rates_ref[...] = -LOG2E * jnp.exp(alog_ref[...])
    return ends


def scan(size_ref, force_ref, vec_ref, rates_ref, mixed_ref, part_ref, hist_ref):
    tokens, channels = size_ref.shape
    width = rates_ref.shape[0]
    tiles = tiles_of(channels)

    def block(b, hidden):
        base = pl.multiple_of(b * 8, 8)
        vectors = pltpu.roll(vec_ref[...], tokens - base, axis=1)
        sizes = size_ref[pl.ds(base, 8), :]
        forces = force_ref[pl.ds(base, 8), :]
        hidden = list(hidden)
        for i in range(8):
            inject = jnp.broadcast_to(vectors[:width, i : i + 1], (width, LANES))
            readout = None
            if mixed_ref is not None:
                readout = jnp.broadcast_to(vectors[width:, i : i + 1], (width, LANES))
            advance(
                hidden, rates_ref, sizes[i : i + 1], forces[i : i + 1], inject, readout,
                part_ref, i * 8,
            )
            if hist_ref is not None:
                for tile, cols in enumerate(tiles):
                    hist_ref[base + i, :, cols] = hidden[tile]
        if mixed_ref is not None:
            mixed_ref[pl.ds(base, 8), :] = gather_sums(part_ref, 0, 8)
        return tuple(hidden)

    zero = jnp.zeros((width, LANES), jnp.float32)
    lax.fori_loop(0, tokens // 8, block, (zero,) * len(tiles), unroll=16)


def states_kernel(
    lengths_ref, routes_ref, proj_ref, x_ref, weight_ref, bias_ref, alog_ref,
    send_ref, size_ref, force_ref, vec_ref, rates_ref, hist_ref, sems,
):
    requests = lengths_ref.shape[1]
    group = lax.axis_index("group")
    proj = proj_ref[...].reshape(x_ref.shape[0], -1)
    ends = prepare_scan(
        lengths_ref, proj, x_ref, weight_ref, bias_ref, alog_ref, size_ref, force_ref, vec_ref,
        rates_ref,
    )
    scan(size_ref, force_ref, vec_ref, rates_ref, None, None, hist_ref)
    dests = [routes_ref[0, group * requests + k] for k in range(requests)]
    copies = []
    for k in range(requests):
        lane = jnp.int32(0)
        for j in range(k):
            lane = lane + (dests[j] == dests[k]).astype(jnp.int32)
        copies.append(
            pltpu.make_async_copy(hist_ref.at[ends[k]], send_ref.at[dests[k], lane], sems.at[k])
        )
        copies[-1].start()
    for copy in copies:
        copy.wait()


def rest_kernel(
    lengths_ref, routes_ref, proj_ref,
    state_hbm, decode_x_hbm, decode_gate_hbm, weight_hbm, alog_hbm, bias_hbm, skip_hbm,
    prefill_x_hbm, prefill_gate_hbm,
    out_ref, mixed_ref, unit_ref, source_ref,
    state_ref, decode_x_ref, decode_gate_ref, weight_ref, alog_ref, bias_ref, skip_ref,
    prefill_x_ref, prefill_gate_ref,
    size_ref, force_ref, act_ref, sum_ref, part_ref, vec_ref, rates_ref, sems, *, groups,
):
    copies = fetch(
        (
            weight_hbm, alog_hbm, bias_hbm, skip_hbm, decode_x_hbm, decode_gate_hbm, state_hbm,
            prefill_x_hbm, prefill_gate_hbm,
        ),
        (
            weight_ref, alog_ref, bias_ref, skip_ref, decode_x_ref, decode_gate_ref, state_ref,
            prefill_x_ref, prefill_gate_ref,
        ),
        sems,
    )
    total, channels = decode_x_ref.shape
    rows, width = state_ref.shape[:2]
    steps = total // rows
    reach = unit_ref.shape[0]
    half = proj_ref.shape[0] // 2
    tiles = tiles_of(channels)
    rank = weight_ref.shape[0]
    requests = lengths_ref.shape[1]
    me = lax.axis_index("group")
    for n in range(reach):
        source_ref[n] = -1
    slot = jnp.int32(0)
    for g in range(groups):
        lane = jnp.int32(0)
        for k in range(requests):
            ours = routes_ref[0, g * requests + k] == me

            @pl.when(ours)
            def _(g=g, slot=slot, lane=lane):
                source_ref[slot] = g * CAP + lane

            slot = slot + ours.astype(jnp.int32)
            lane = lane + ours.astype(jnp.int32)

    for copy in copies[:5]:
        copy.wait()
    proj = proj_ref[half:].reshape(total, -1)
    size = step_sizes(proj, weight_ref, bias_ref)
    values = decode_x_ref[...].astype(jnp.float32)
    size_ref[...] = size
    force_ref[...] = size * values
    vec_ref[...] = jnp.transpose(proj[:, rank:])
    rates_ref[...] = -LOG2E * jnp.exp(alog_ref[...])
    copies[5].wait()
    act_ref[...] = silu(decode_gate_ref[...].astype(jnp.float32))
    copies[6].wait()

    def block(b, carry, units):
        base = pl.multiple_of(b * 8, 8)
        at = [pl.multiple_of(s * rows + base, 8) for s in range(steps)]
        vectors = [pltpu.roll(vec_ref[...], total - at[s], axis=1) for s in range(steps)]
        sizes = [size_ref[pl.ds(at[s], 8), :] for s in range(steps)]
        forces = [force_ref[pl.ds(at[s], 8), :] for s in range(steps)]
        acts = [act_ref[pl.ds(at[s], 8), :] for s in range(steps)]
        for i in range(8):
            hidden = [state_ref[base + i, :, cols] for cols in tiles]
            if units:
                taken = source_ref[base + i] >= 0
                hidden = [jnp.where(taken, 0.0, start) for start in hidden]
            summed = None
            for s in range(steps):
                inject = jnp.broadcast_to(vectors[s][:width, i : i + 1], (width, LANES))
                readout = jnp.broadcast_to(vectors[s][width:, i : i + 1], (width, LANES))
                row = sizes[s][i : i + 1]
                advance(
                    hidden, rates_ref, row, forces[s][i : i + 1], inject, readout, part_ref,
                    (s * 8 + i) * 8,
                )
                if units:
                    summed = row if s == 0 else summed + row
                    for cols in tiles:
                        unit_ref[base + i, s, :, cols] = (
                            readout * acts[s][i : i + 1, cols]
                        ) * jnp.exp2(summed[:, cols] * rates_ref[:, cols])
        for s in range(steps):
            sum_ref[pl.ds(at[s], 8), :] = gather_sums(part_ref, s * 64, 8)
        return carry

    lax.fori_loop(0, reach // 8, functools.partial(block, units=True), 0)
    lax.fori_loop(reach // 8, rows // 8, functools.partial(block, units=False), 0)
    mixed_ref[...] = (sum_ref[...] + skip_ref[...] * values) * act_ref[...]

    copies[7].wait()
    proj = proj_ref[:half].reshape(total, -1)
    prepare_scan(
        lengths_ref, proj, prefill_x_ref, weight_ref, bias_ref, alog_ref, size_ref, force_ref,
        vec_ref, rates_ref,
    )
    scan(size_ref, force_ref, vec_ref, rates_ref, sum_ref, part_ref, None)
    copies[8].wait()
    mixed = sum_ref[...] + skip_ref[...] * prefill_x_ref[...].astype(jnp.float32)
    out_ref[...] = (mixed * silu(prefill_gate_ref[...].astype(jnp.float32))).astype(out_ref.dtype)


def combine_kernel(source_ref, mixed_ref, unit_ref, recv_ref, out_ref):
    reach, steps = unit_ref.shape[:2]
    rows = mixed_ref.shape[0] // steps
    added = [[] for _ in range(steps)]
    for n in range(reach):
        source = source_ref[n]
        state = jnp.where(source >= 0, recv_ref[jnp.maximum(source, 0)], 0.0)
        for s in range(steps):
            added[s].append(jnp.sum(unit_ref[n, s] * state, axis=0, keepdims=True))
    for s in range(steps):
        first, last = s * rows, (s + 1) * rows
        out_ref[first : first + reach, :] = (
            mixed_ref[first : first + reach, :] + jnp.concatenate(added[s], axis=0)
        ).astype(out_ref.dtype)
        out_ref[first + reach : last, :] = mixed_ref[first + reach : last, :].astype(out_ref.dtype)


def local(
    prefill_x, prefill_gate, lengths, routes, decode_x, decode_gate, cached_state, xproj_weight,
    dt_weight, dt_bias, a_log, skip_gain, *, ranks, groups,
):
    tokens, channels = prefill_x.shape
    steps, rows, _ = decode_x.shape
    width = a_log.shape[0]
    requests = lengths.shape[1]
    columns = xproj_weight.shape[1]
    total = steps * rows
    reach = groups * CAP
    decode_flat = decode_x.reshape(total, channels)
    gate_flat = decode_gate.reshape(total, channels)
    bias = dt_bias.reshape(1, channels)
    skip = skip_gain.reshape(1, channels)
    per = (tokens + total) // ranks
    routes = routes.T
    chunked = struct((ranks, per, columns))

    partial = call(
        project_kernel, "project", chunked, [ANY] * 3,
        scratch=[
            bf16(columns, channels), bf16(tokens, channels), bf16(total, channels),
            pltpu.SemaphoreType.DMA((3,)),
        ],
    )(*stay(xproj_weight.T, prefill_x, decode_flat))
    parts = lax.all_to_all(partial, "tp", 0, 0)
    copies = call(total_kernel, "total", chunked, [VMEM])(parts)
    proj = lax.all_to_all(copies, "tp", 0, 0)

    scan_scratch = [
        f32(tokens, channels), f32(tokens, channels), f32(2 * width, tokens), f32(width, channels)
    ]
    send = call(
        states_kernel, "states", struct((groups, CAP, width, channels)),
        [SMEM, SMEM, pl.BlockSpec((ranks // 2, per, columns), lambda i: (0, 0, 0))] + [VMEM] * 4,
        out_specs=ANY,
        scratch=scan_scratch
        + [f32(tokens, width, channels), pltpu.SemaphoreType.DMA((requests,))],
    )(lengths, routes, proj, prefill_x, dt_weight, bias, a_log)
    recv = lax.all_to_all(send, "group", 0, 0)
    prefill_out, mixed, unit, source = call(
        functools.partial(rest_kernel, groups=groups), "rest",
        (
            struct((tokens, channels), jnp.bfloat16), struct((total, channels)),
            struct((reach, steps, width, channels)), struct((reach,), jnp.int32),
        ),
        [SMEM, SMEM, VMEM] + [ANY] * 9,
        out_specs=(VMEM, VMEM, VMEM, SMEM),
        scratch=[
            f32(rows, width, channels), bf16(total, channels), bf16(total, channels),
            bf16(*dt_weight.shape), f32(width, channels), f32(1, channels), f32(1, channels),
            bf16(tokens, channels), bf16(tokens, channels),
            f32(total, channels), f32(total, channels), f32(total, channels),
            f32(total, channels), f32(channels // LANES, steps * 64, LANES), f32(2 * width, total),
            f32(width, channels), pltpu.SemaphoreType.DMA((9,)),
        ],
        flops=8 * 10**9,
    )(
        lengths, routes, proj,
        *stay(
            cached_state, decode_flat, gate_flat, dt_weight, a_log, bias, skip, prefill_x,
            prefill_gate,
        ),
    )
    decode_out = call(
        combine_kernel, "combine", struct((total, channels), jnp.bfloat16), [SMEM] + [VMEM] * 3
    )(source, mixed, unit, recv.reshape(reach, width, channels))
    return prefill_out, decode_out.reshape(steps, rows, channels)


def solution(mesh):
    placed = (
        P("group", "tp"), P("group", "tp"), P("group", None), P(), P(None, "group", "tp"),
        P(None, "group", "tp"), P("group", None, "tp"), P("tp", None), P(None, "tp"), P("tp"),
        P(None, "tp"), P("tp"),
    )
    body = functools.partial(local, ranks=mesh.shape["tp"], groups=mesh.shape["group"])
    return jax.shard_map(
        body, mesh=mesh, in_specs=placed, out_specs=(P("group", "tp"), P(None, "group", "tp")),
        check_vma=False,
    )
```

```python
import functools

import jax
import jax.numpy as jnp
from jax import lax
from jax.experimental import pallas as pl
from jax.experimental.pallas import tpu as pltpu
from jax.sharding import PartitionSpec as P

LOG2E = 1.4426950408889634
FAR = 1e30
LANES = 128
CAP = 2

VMEM = pl.BlockSpec(memory_space=pltpu.VMEM)
SMEM = pl.BlockSpec(memory_space=pltpu.SMEM)
ANY = pl.BlockSpec(memory_space=pl.ANY)


def call(kernel, name, out_shape, in_specs, out_specs=VMEM, scratch=(), mib=16, flops=0):
    return pl.pallas_call(
        kernel,
        grid=(1,),
        out_shape=out_shape,
        in_specs=in_specs,
        out_specs=out_specs,
        scratch_shapes=scratch,
        compiler_params=pltpu.CompilerParams(vmem_limit_bytes=mib << 20),
        cost_estimate=pl.CostEstimate(flops=flops, bytes_accessed=1 << 20, transcendentals=0),
        name=name,
    )


def f32(*shape):
    return pltpu.VMEM(shape, jnp.float32)


def bf16(*shape):
    return pltpu.VMEM(shape, jnp.bfloat16)


def struct(shape, dtype=jnp.float32):
    return jax.ShapeDtypeStruct(shape, dtype)


def stay(*arrays):
    return tuple(pltpu.with_memory_space_constraint(a, pltpu.HBM) for a in arrays)


def fetch(sources, targets, sems):
    copies = [
        pltpu.make_async_copy(a, b, sems.at[i]) for i, (a, b) in enumerate(zip(sources, targets))
    ]
    for copy in copies:
        copy.start()
    return copies


def softplus(v):
    return jnp.maximum(v, 0.0) + jnp.log1p(jnp.exp(-jnp.abs(v)))


def silu(v):
    return v / (1.0 + jnp.exp(-v))


def tiles_of(channels):
    return [slice(t, t + LANES) for t in range(0, channels, LANES)]


def low_rows(rank, j, tile):
    first = j * (8 * (rank // LANES) + 2) + 8 * tile
    return slice(first, first + 8)


def vector_rows(rank, count, which):
    height = 8 * (rank // LANES) + 2
    return pl.ds(height - 2 + which, count, stride=height)


def low_part(proj_ref, rank, half, which):
    tiles = range(rank // LANES)
    return jnp.concatenate(
        [
            jnp.concatenate([proj_ref[low_rows(rank, j, tile), :] for tile in tiles], axis=1)
            for j in range(half * which, half * (which + 1))
        ],
        axis=0,
    )


def project_kernel(
    weight_hbm, prefill_hbm, decode_hbm, out_ref, weight_ref, prefill_ref, decode_ref, sems,
    *, rank,
):
    copies = fetch(
        (weight_hbm, prefill_hbm, decode_hbm), (weight_ref, prefill_ref, decode_ref), sems
    )
    count = weight_ref.shape[0] - rank
    half = count // 2
    copies[0].wait()
    for which, ref in enumerate((prefill_ref, decode_ref)):
        copies[which + 1].wait()
        values = ref[...]
        low = lax.dot_general(
            values, weight_ref[:rank], (((1,), (1,)), ((), ())), preferred_element_type=jnp.float32
        )
        for j in range(half):
            for tile, cols in enumerate(tiles_of(rank)):
                out_ref[low_rows(rank, half * which + j, tile), :] = low[8 * j : 8 * j + 8, cols]
        out_ref[vector_rows(rank, count, which), :] = lax.dot_general(
            weight_ref[rank:], values, (((1,), (1,)), ((), ())), preferred_element_type=jnp.float32
        )


def total_kernel(parts_ref, out_ref, *, ranks):
    height = parts_ref.shape[0] // ranks
    group = 4
    quad = parts_ref[...].reshape(ranks // group, group * height, LANES).sum(axis=0)
    total = quad[:height]
    for i in range(1, group):
        total = total + quad[i * height : (i + 1) * height]
    quad = jnp.concatenate([total] * group, axis=0)
    for i in range(ranks // group):
        out_ref[i * group * height : (i + 1) * group * height, :] = quad


def step_sizes(low, weight_ref, bias_ref):
    low = low.astype(jnp.bfloat16)
    return softplus(
        jnp.dot(low, weight_ref[...], preferred_element_type=jnp.float32) + bias_ref[...]
    )


def fold(terms):
    return sum(terms[i : i + 8] for i in range(8, terms.shape[0], 8)) + terms[:8]


def gather_sums(part_ref, first, stride):
    return jnp.concatenate(
        [
            sum(
                (part_ref[tile, pl.ds(first + j, 8, stride=stride), :] for j in range(1, 8)),
                part_ref[tile, pl.ds(first, 8, stride=stride), :],
            )
            for tile in range(part_ref.shape[0])
        ],
        axis=1,
    )


def advance(hidden, rates_ref, size_row, forcing_row, inject, readout, part_ref, at):
    for tile, cols in enumerate(tiles_of(size_row.shape[1])):
        damping = jnp.exp2(size_row[:, cols] * rates_ref[:, cols])
        hidden[tile] = damping * hidden[tile] + forcing_row[:, cols] * inject
        if readout is not None:
            part_ref[tile, at : at + 8, :] = fold(readout * hidden[tile])


def prepare_scan(lengths_ref, proj_ref, x_ref, weight_ref, bias_ref, alog_ref, size_ref, force_ref, vec_ref, rates_ref):
    tokens, channels = x_ref.shape
    rank = weight_ref.shape[0]
    count = vec_ref.shape[0]
    low = low_part(proj_ref, rank, count // 2, 0)
    size = step_sizes(low, weight_ref, bias_ref)
    force_ref[...] = size * x_ref[...].astype(jnp.float32)
    position = lax.broadcasted_iota(jnp.int32, (tokens, LANES), 0)
    first = position == 0
    begin = jnp.int32(0)
    ends = []
    for k in range(lengths_ref.shape[1]):
        first = first | (position == begin)
        begin = begin + lengths_ref[0, k]
        ends.append(begin - 1)
    reset = jnp.where(first, jnp.float32(FAR), jnp.float32(0.0))
    for cols in tiles_of(channels):
        size_ref[:, cols] = size[:, cols] + reset
    vec_ref[...] = proj_ref[vector_rows(rank, count, 0), :]
    rates_ref[...] = -LOG2E * jnp.exp(alog_ref[...])
    return ends


def scan(size_ref, force_ref, vec_ref, rates_ref, mixed_ref, part_ref, hist_ref):
    tokens, channels = size_ref.shape
    width = rates_ref.shape[0]
    tiles = tiles_of(channels)

    def block(b, hidden):
        base = pl.multiple_of(b * 8, 8)
        vectors = pltpu.roll(vec_ref[...], tokens - base, axis=1)
        sizes = size_ref[pl.ds(base, 8), :]
        forces = force_ref[pl.ds(base, 8), :]
        hidden = list(hidden)
        for i in range(8):
            inject = jnp.broadcast_to(vectors[:width, i : i + 1], (width, LANES))
            readout = None
            if mixed_ref is not None:
                readout = jnp.broadcast_to(vectors[width:, i : i + 1], (width, LANES))
            advance(
                hidden, rates_ref, sizes[i : i + 1], forces[i : i + 1], inject, readout,
                part_ref, i * 8,
            )
            if hist_ref is not None:
                for tile, cols in enumerate(tiles):
                    hist_ref[base + i, :, cols] = hidden[tile]
        if mixed_ref is not None:
            mixed_ref[pl.ds(base, 8), :] = gather_sums(part_ref, 0, 8)
        return tuple(hidden)

    zero = jnp.zeros((width, LANES), jnp.float32)
    lax.fori_loop(0, tokens // 8, block, (zero,) * len(tiles), unroll=16)


def states_kernel(
    lengths_ref, routes_ref, proj_ref, x_ref, weight_ref, bias_ref, alog_ref,
    send_ref, size_ref, force_ref, vec_ref, rates_ref, hist_ref, sems,
):
    requests = lengths_ref.shape[1]
    group = lax.axis_index("group")
    ends = prepare_scan(
        lengths_ref, proj_ref, x_ref, weight_ref, bias_ref, alog_ref, size_ref, force_ref, vec_ref,
        rates_ref,
    )
    scan(size_ref, force_ref, vec_ref, rates_ref, None, None, hist_ref)
    dests = [routes_ref[0, group * requests + k] for k in range(requests)]
    copies = []
    for k in range(requests):
        lane = jnp.int32(0)
        for j in range(k):
            lane = lane + (dests[j] == dests[k]).astype(jnp.int32)
        copies.append(
            pltpu.make_async_copy(hist_ref.at[ends[k]], send_ref.at[dests[k], lane], sems.at[k])
        )
        copies[-1].start()
    for copy in copies:
        copy.wait()


def rest_kernel(
    lengths_ref, routes_ref, proj_ref,
    state_hbm, decode_x_hbm, decode_gate_hbm, weight_hbm, alog_hbm, bias_hbm, skip_hbm,
    prefill_x_hbm, prefill_gate_hbm,
    out_ref, mixed_ref, unit_ref, source_ref,
    state_ref, decode_x_ref, decode_gate_ref, weight_ref, alog_ref, bias_ref, skip_ref,
    prefill_x_ref, prefill_gate_ref,
    size_ref, force_ref, act_ref, sum_ref, part_ref, vec_ref, rates_ref, sems, *, groups,
):
    copies = fetch(
        (
            weight_hbm, alog_hbm, bias_hbm, skip_hbm, decode_x_hbm, decode_gate_hbm, state_hbm,
            prefill_x_hbm, prefill_gate_hbm,
        ),
        (
            weight_ref, alog_ref, bias_ref, skip_ref, decode_x_ref, decode_gate_ref, state_ref,
            prefill_x_ref, prefill_gate_ref,
        ),
        sems,
    )
    total, channels = decode_x_ref.shape
    rows, width = state_ref.shape[:2]
    steps = total // rows
    reach = unit_ref.shape[0]
    tiles = tiles_of(channels)
    rank = weight_ref.shape[0]
    count = vec_ref.shape[0]
    requests = lengths_ref.shape[1]
    me = lax.axis_index("group")
    for n in range(reach):
        source_ref[n] = -1
    slot = jnp.int32(0)
    for g in range(groups):
        lane = jnp.int32(0)
        for k in range(requests):
            ours = routes_ref[0, g * requests + k] == me

            @pl.when(ours)
            def _(g=g, slot=slot, lane=lane):
                source_ref[slot] = g * CAP + lane

            slot = slot + ours.astype(jnp.int32)
            lane = lane + ours.astype(jnp.int32)

    for copy in copies[:5]:
        copy.wait()
    size = step_sizes(low_part(proj_ref, rank, count // 2, 1), weight_ref, bias_ref)
    values = decode_x_ref[...].astype(jnp.float32)
    size_ref[...] = size
    force_ref[...] = size * values
    vec_ref[...] = proj_ref[vector_rows(rank, count, 1), :]
    rates_ref[...] = -LOG2E * jnp.exp(alog_ref[...])
    copies[5].wait()
    act_ref[...] = silu(decode_gate_ref[...].astype(jnp.float32))
    copies[6].wait()

    def block(b, carry, units):
        base = pl.multiple_of(b * 8, 8)
        at = [pl.multiple_of(s * rows + base, 8) for s in range(steps)]
        vectors = [pltpu.roll(vec_ref[...], total - at[s], axis=1) for s in range(steps)]
        sizes = [size_ref[pl.ds(at[s], 8), :] for s in range(steps)]
        forces = [force_ref[pl.ds(at[s], 8), :] for s in range(steps)]
        acts = [act_ref[pl.ds(at[s], 8), :] for s in range(steps)]
        for i in range(8):
            hidden = [state_ref[base + i, :, cols] for cols in tiles]
            if units:
                taken = source_ref[base + i] >= 0
                hidden = [jnp.where(taken, 0.0, start) for start in hidden]
            summed = None
            for s in range(steps):
                inject = jnp.broadcast_to(vectors[s][:width, i : i + 1], (width, LANES))
                readout = jnp.broadcast_to(vectors[s][width:, i : i + 1], (width, LANES))
                row = sizes[s][i : i + 1]
                advance(
                    hidden, rates_ref, row, forces[s][i : i + 1], inject, readout, part_ref,
                    (s * 8 + i) * 8,
                )
                if units:
                    summed = row if s == 0 else summed + row
                    for cols in tiles:
                        unit_ref[base + i, s, :, cols] = (
                            readout * acts[s][i : i + 1, cols]
                        ) * jnp.exp2(summed[:, cols] * rates_ref[:, cols])
        for s in range(steps):
            sum_ref[pl.ds(at[s], 8), :] = gather_sums(part_ref, s * 64, 8)
        return carry

    lax.fori_loop(0, reach // 8, functools.partial(block, units=True), 0)
    lax.fori_loop(reach // 8, rows // 8, functools.partial(block, units=False), 0)
    mixed_ref[...] = (sum_ref[...] + skip_ref[...] * values) * act_ref[...]

    copies[7].wait()
    prepare_scan(
        lengths_ref, proj_ref, prefill_x_ref, weight_ref, bias_ref, alog_ref, size_ref, force_ref,
        vec_ref, rates_ref,
    )
    scan(size_ref, force_ref, vec_ref, rates_ref, sum_ref, part_ref, None)
    copies[8].wait()
    mixed = sum_ref[...] + skip_ref[...] * prefill_x_ref[...].astype(jnp.float32)
    out_ref[...] = (mixed * silu(prefill_gate_ref[...].astype(jnp.float32))).astype(out_ref.dtype)


def combine_kernel(source_ref, mixed_ref, unit_ref, recv_ref, out_ref):
    reach, steps = unit_ref.shape[:2]
    rows = mixed_ref.shape[0] // steps
    added = [[] for _ in range(steps)]
    for n in range(reach):
        source = source_ref[n]
        state = jnp.where(source >= 0, recv_ref[jnp.maximum(source, 0)], 0.0)
        for s in range(steps):
            added[s].append(jnp.sum(unit_ref[n, s] * state, axis=0, keepdims=True))
    for s in range(steps):
        first, last = s * rows, (s + 1) * rows
        out_ref[first : first + reach, :] = (
            mixed_ref[first : first + reach, :] + jnp.concatenate(added[s], axis=0)
        ).astype(out_ref.dtype)
        out_ref[first + reach : last, :] = mixed_ref[first + reach : last, :].astype(out_ref.dtype)


def local(
    prefill_x, prefill_gate, lengths, routes, decode_x, decode_gate, cached_state, xproj_weight,
    dt_weight, dt_bias, a_log, skip_gain, *, ranks, groups,
):
    tokens, channels = prefill_x.shape
    steps, rows, _ = decode_x.shape
    width = a_log.shape[0]
    requests = lengths.shape[1]
    columns = xproj_weight.shape[1]
    total = steps * rows
    reach = groups * CAP
    decode_flat = decode_x.reshape(total, channels)
    gate_flat = decode_gate.reshape(total, channels)
    bias = dt_bias.reshape(1, channels)
    skip = skip_gain.reshape(1, channels)
    rank = dt_weight.shape[0]
    height = 8 * (rank // LANES) + 2
    routes = routes.T
    flat = struct((ranks * height, LANES))

    def exchange(rows):
        chunks = rows.reshape(ranks, height // 2, 2, LANES)
        return lax.all_to_all(chunks, "tp", 0, 0).reshape(ranks * height, LANES)

    partial = call(
        functools.partial(project_kernel, rank=rank), "project", flat, [ANY] * 3,
        scratch=[
            bf16(columns, channels), bf16(tokens, channels), bf16(total, channels),
            pltpu.SemaphoreType.DMA((3,)),
        ],
    )(*stay(xproj_weight.T, prefill_x, decode_flat))
    copies = call(functools.partial(total_kernel, ranks=ranks), "total", flat, [VMEM])(
        exchange(partial)
    )
    proj = exchange(copies)

    scan_scratch = [
        f32(tokens, channels), f32(tokens, channels), f32(2 * width, tokens), f32(width, channels)
    ]
    send = call(
        states_kernel, "states", struct((groups, CAP, width, channels)),
        [SMEM, SMEM] + [VMEM] * 5,
        out_specs=ANY,
        scratch=scan_scratch
        + [f32(tokens, width, channels), pltpu.SemaphoreType.DMA((requests,))],
    )(lengths, routes, proj, prefill_x, dt_weight, bias, a_log)
    recv = lax.all_to_all(send, "group", 0, 0)
    prefill_out, mixed, unit, source = call(
        functools.partial(rest_kernel, groups=groups), "rest",
        (
            struct((tokens, channels), jnp.bfloat16), struct((total, channels)),
            struct((reach, steps, width, channels)), struct((reach,), jnp.int32),
        ),
        [SMEM, SMEM, VMEM] + [ANY] * 9,
        out_specs=(VMEM, VMEM, VMEM, SMEM),
        scratch=[
            f32(rows, width, channels), bf16(total, channels), bf16(total, channels),
            bf16(*dt_weight.shape), f32(width, channels), f32(1, channels), f32(1, channels),
            bf16(tokens, channels), bf16(tokens, channels),
            f32(total, channels), f32(total, channels), f32(total, channels),
            f32(total, channels), f32(channels // LANES, steps * 64, LANES), f32(2 * width, total),
            f32(width, channels), pltpu.SemaphoreType.DMA((9,)),
        ],
        flops=8 * 10**9,
    )(
        lengths, routes, proj,
        *stay(
            cached_state, decode_flat, gate_flat, dt_weight, a_log, bias, skip, prefill_x,
            prefill_gate,
        ),
    )
    decode_out = call(
        combine_kernel, "combine", struct((total, channels), jnp.bfloat16), [SMEM] + [VMEM] * 3
    )(source, mixed, unit, recv.reshape(reach, width, channels))
    return prefill_out, decode_out.reshape(steps, rows, channels)


def solution(mesh):
    placed = (
        P("group", "tp"), P("group", "tp"), P("group", None), P(), P(None, "group", "tp"),
        P(None, "group", "tp"), P("group", None, "tp"), P("tp", None), P(None, "tp"), P("tp"),
        P(None, "tp"), P("tp"),
    )
    body = functools.partial(local, ranks=mesh.shape["tp"], groups=mesh.shape["group"])
    return jax.shard_map(
        body, mesh=mesh, in_specs=placed, out_specs=(P("group", "tp"), P(None, "group", "tp")),
        check_vma=False,
    )
```

```python
import functools

import jax
import jax.numpy as jnp
from jax import lax
from jax.experimental import pallas as pl
from jax.experimental.pallas import tpu as pltpu
from jax.sharding import PartitionSpec as P

LOG2E = 1.4426950408889634
FAR = 1e30
LANES = 128
CAP = 2

VMEM = pl.BlockSpec(memory_space=pltpu.VMEM)
SMEM = pl.BlockSpec(memory_space=pltpu.SMEM)
ANY = pl.BlockSpec(memory_space=pl.ANY)


def call(kernel, name, out_shape, in_specs, out_specs=VMEM, scratch=(), mib=16, flops=0):
    return pl.pallas_call(
        kernel,
        grid=(1,),
        out_shape=out_shape,
        in_specs=in_specs,
        out_specs=out_specs,
        scratch_shapes=scratch,
        compiler_params=pltpu.CompilerParams(vmem_limit_bytes=mib << 20),
        cost_estimate=pl.CostEstimate(flops=flops, bytes_accessed=1 << 20, transcendentals=0),
        name=name,
    )


def f32(*shape):
    return pltpu.VMEM(shape, jnp.float32)


def bf16(*shape):
    return pltpu.VMEM(shape, jnp.bfloat16)


def struct(shape, dtype=jnp.float32):
    return jax.ShapeDtypeStruct(shape, dtype)


def stay(*arrays):
    return tuple(pltpu.with_memory_space_constraint(a, pltpu.HBM) for a in arrays)


def fetch(sources, targets, sems):
    copies = [
        pltpu.make_async_copy(a, b, sems.at[i]) for i, (a, b) in enumerate(zip(sources, targets))
    ]
    for copy in copies:
        copy.start()
    return copies


def softplus(v):
    return jnp.maximum(v, 0.0) + jnp.log1p(jnp.exp(-jnp.abs(v)))


def silu(v):
    return v / (1.0 + jnp.exp(-v))


def tiles_of(channels):
    return [slice(t, t + LANES) for t in range(0, channels, LANES)]


def low_rows(rank, j, tile):
    first = j * (8 * (rank // LANES) + 2) + 8 * tile
    return slice(first, first + 8)


def vector_rows(rank, count, which):
    height = 8 * (rank // LANES) + 2
    return pl.ds(height - 2 + which, count, stride=height)


def low_part(proj_ref, rank, half, which):
    tiles = range(rank // LANES)
    return jnp.concatenate(
        [
            jnp.concatenate([proj_ref[low_rows(rank, j, tile), :] for tile in tiles], axis=1)
            for j in range(half * which, half * (which + 1))
        ],
        axis=0,
    )


def project_kernel(
    weight_hbm, prefill_hbm, decode_hbm, out_ref, weight_ref, prefill_ref, decode_ref, sems,
    *, rank,
):
    copies = fetch(
        (weight_hbm, prefill_hbm, decode_hbm), (weight_ref, prefill_ref, decode_ref), sems
    )
    count = weight_ref.shape[0] - rank
    half = count // 2
    copies[0].wait()
    for which, ref in enumerate((prefill_ref, decode_ref)):
        copies[which + 1].wait()
        values = ref[...]
        low = lax.dot_general(
            values, weight_ref[:rank], (((1,), (1,)), ((), ())), preferred_element_type=jnp.float32
        )
        for j in range(half):
            for tile, cols in enumerate(tiles_of(rank)):
                out_ref[low_rows(rank, half * which + j, tile), :] = low[8 * j : 8 * j + 8, cols]
        out_ref[vector_rows(rank, count, which), :] = lax.dot_general(
            weight_ref[rank:], values, (((1,), (1,)), ((), ())), preferred_element_type=jnp.float32
        )


def total_kernel(parts_ref, out_ref, *, ranks):
    height = parts_ref.shape[0] // ranks
    group = 4
    quad = parts_ref[...].reshape(ranks // group, group * height, LANES).sum(axis=0)
    total = quad[:height]
    for i in range(1, group):
        total = total + quad[i * height : (i + 1) * height]
    quad = jnp.concatenate([total] * group, axis=0)
    for i in range(ranks // group):
        out_ref[i * group * height : (i + 1) * group * height, :] = quad


def step_sizes(low, weight_ref, bias_ref):
    low = low.astype(jnp.bfloat16)
    return softplus(
        jnp.dot(low, weight_ref[...], preferred_element_type=jnp.float32) + bias_ref[...]
    )


def fold(terms):
    return sum(terms[i : i + 8] for i in range(8, terms.shape[0], 8)) + terms[:8]


def gather_sums(part_ref, first, stride):
    return jnp.concatenate(
        [
            sum(
                (part_ref[tile, pl.ds(first + j, 8, stride=stride), :] for j in range(1, 8)),
                part_ref[tile, pl.ds(first, 8, stride=stride), :],
            )
            for tile in range(part_ref.shape[0])
        ],
        axis=1,
    )


def advance(hidden, rates_ref, size_row, forcing_row, inject, readout, part_ref, at):
    for tile, cols in enumerate(tiles_of(size_row.shape[1])):
        damping = jnp.exp2(size_row[:, cols] * rates_ref[:, cols])
        hidden[tile] = damping * hidden[tile] + forcing_row[:, cols] * inject
        if readout is not None:
            part_ref[tile, at : at + 8, :] = fold(readout * hidden[tile])


def prepare_scan(lengths_ref, proj_ref, x_ref, weight_ref, bias_ref, alog_ref, size_ref, force_ref, vec_ref, rates_ref):
    tokens, channels = x_ref.shape
    rank = weight_ref.shape[0]
    count = vec_ref.shape[0]
    low = low_part(proj_ref, rank, count // 2, 0)
    size = step_sizes(low, weight_ref, bias_ref)
    force_ref[...] = size * x_ref[...].astype(jnp.float32)
    position = lax.broadcasted_iota(jnp.int32, (tokens, LANES), 0)
    first = position == 0
    begin = jnp.int32(0)
    ends = []
    for k in range(lengths_ref.shape[1]):
        first = first | (position == begin)
        begin = begin + lengths_ref[0, k]
        ends.append(begin - 1)
    reset = jnp.where(first, jnp.float32(FAR), jnp.float32(0.0))
    for cols in tiles_of(channels):
        size_ref[:, cols] = size[:, cols] + reset
    vec_ref[...] = proj_ref[vector_rows(rank, count, 0), :]
    rates_ref[...] = -LOG2E * jnp.exp(alog_ref[...])
    return ends


def scan(size_ref, force_ref, vec_ref, rates_ref, mixed_ref, part_ref, hist_ref):
    tokens, channels = size_ref.shape
    width = rates_ref.shape[0]
    tiles = tiles_of(channels)

    def block(b, hidden):
        base = pl.multiple_of(b * 8, 8)
        vectors = pltpu.roll(vec_ref[...], tokens - base, axis=1)
        sizes = size_ref[pl.ds(base, 8), :]
        forces = force_ref[pl.ds(base, 8), :]
        hidden = list(hidden)
        for i in range(8):
            inject = jnp.broadcast_to(vectors[:width, i : i + 1], (width, LANES))
            readout = None
            if mixed_ref is not None:
                readout = jnp.broadcast_to(vectors[width:, i : i + 1], (width, LANES))
            advance(
                hidden, rates_ref, sizes[i : i + 1], forces[i : i + 1], inject, readout,
                part_ref, i * 8,
            )
            if hist_ref is not None:
                for tile, cols in enumerate(tiles):
                    hist_ref[base + i, :, cols] = hidden[tile]
        if mixed_ref is not None:
            mixed_ref[pl.ds(base, 8), :] = gather_sums(part_ref, 0, 8)
        return tuple(hidden)

    zero = jnp.zeros((width, LANES), jnp.float32)
    lax.fori_loop(0, tokens // 8, block, (zero,) * len(tiles), unroll=16)


def states_kernel(
    lengths_ref, routes_ref, proj_ref, x_ref, weight_ref, bias_ref, alog_ref,
    *rest,
):
    send_refs, (size_ref, force_ref, vec_ref, rates_ref, hist_ref, send_ref) = rest[:-6], rest[-6:]
    chips = len(send_refs)
    requests = lengths_ref.shape[1]
    group = lax.axis_index("group")
    ends = prepare_scan(
        lengths_ref, proj_ref, x_ref, weight_ref, bias_ref, alog_ref, size_ref, force_ref, vec_ref,
        rates_ref,
    )
    scan(size_ref, force_ref, vec_ref, rates_ref, None, None, hist_ref)
    dests = [routes_ref[0, group * requests + k] for k in range(requests)]
    for k in range(requests):
        lane = jnp.int32(0)
        for j in range(k):
            lane = lane + (dests[j] == dests[k]).astype(jnp.int32)
        ahead = lax.rem(dests[k] // 2 - group // 2 + chips, chips)
        other = lax.rem(dests[k] + group, 2)
        send_ref[ahead, other, lane] = hist_ref[ends[k]]
    for chip in range(chips):
        send_refs[chip][...] = send_ref[chip]


def rest_kernel(
    lengths_ref, routes_ref, proj_ref,
    state_hbm, decode_x_hbm, decode_gate_hbm, weight_hbm, alog_hbm, bias_hbm, skip_hbm,
    prefill_x_hbm, prefill_gate_hbm,
    out_ref, mixed_ref, unit_ref, source_ref,
    state_ref, decode_x_ref, decode_gate_ref, weight_ref, alog_ref, bias_ref, skip_ref,
    prefill_x_ref, prefill_gate_ref,
    size_ref, force_ref, act_ref, sum_ref, part_ref, vec_ref, rates_ref, sems, *, groups,
):
    copies = fetch(
        (
            weight_hbm, alog_hbm, bias_hbm, skip_hbm, decode_x_hbm, decode_gate_hbm, state_hbm,
            prefill_x_hbm, prefill_gate_hbm,
        ),
        (
            weight_ref, alog_ref, bias_ref, skip_ref, decode_x_ref, decode_gate_ref, state_ref,
            prefill_x_ref, prefill_gate_ref,
        ),
        sems,
    )
    total, channels = decode_x_ref.shape
    rows, width = state_ref.shape[:2]
    steps = total // rows
    reach = unit_ref.shape[0]
    tiles = tiles_of(channels)
    rank = weight_ref.shape[0]
    count = vec_ref.shape[0]
    requests = lengths_ref.shape[1]
    me = lax.axis_index("group")
    for n in range(reach):
        source_ref[n] = -1
    slot = jnp.int32(0)
    for g in range(groups):
        lane = jnp.int32(0)
        for k in range(requests):
            ours = routes_ref[0, g * requests + k] == me

            @pl.when(ours)
            def _(g=g, slot=slot, lane=lane):
                behind = lax.rem(me // 2 - g // 2 + groups // 2, groups // 2)
                source_ref[slot] = (behind * 2 + lax.rem(me + g, 2)) * CAP + lane

            slot = slot + ours.astype(jnp.int32)
            lane = lane + ours.astype(jnp.int32)

    for copy in copies[:5]:
        copy.wait()
    size = step_sizes(low_part(proj_ref, rank, count // 2, 1), weight_ref, bias_ref)
    values = decode_x_ref[...].astype(jnp.float32)
    size_ref[...] = size
    force_ref[...] = size * values
    vec_ref[...] = proj_ref[vector_rows(rank, count, 1), :]
    rates_ref[...] = -LOG2E * jnp.exp(alog_ref[...])
    copies[5].wait()
    act_ref[...] = silu(decode_gate_ref[...].astype(jnp.float32))
    copies[6].wait()

    def block(b, carry, units):
        base = pl.multiple_of(b * 8, 8)
        at = [pl.multiple_of(s * rows + base, 8) for s in range(steps)]
        vectors = [pltpu.roll(vec_ref[...], total - at[s], axis=1) for s in range(steps)]
        sizes = [size_ref[pl.ds(at[s], 8), :] for s in range(steps)]
        forces = [force_ref[pl.ds(at[s], 8), :] for s in range(steps)]
        acts = [act_ref[pl.ds(at[s], 8), :] for s in range(steps)]
        for i in range(8):
            hidden = [state_ref[base + i, :, cols] for cols in tiles]
            if units:
                taken = source_ref[base + i] >= 0
                hidden = [jnp.where(taken, 0.0, start) for start in hidden]
            summed = None
            for s in range(steps):
                inject = jnp.broadcast_to(vectors[s][:width, i : i + 1], (width, LANES))
                readout = jnp.broadcast_to(vectors[s][width:, i : i + 1], (width, LANES))
                row = sizes[s][i : i + 1]
                advance(
                    hidden, rates_ref, row, forces[s][i : i + 1], inject, readout, part_ref,
                    (s * 8 + i) * 8,
                )
                if units:
                    summed = row if s == 0 else summed + row
                    for cols in tiles:
                        unit_ref[base + i, s, :, cols] = (
                            readout * acts[s][i : i + 1, cols]
                        ) * jnp.exp2(summed[:, cols] * rates_ref[:, cols])
        for s in range(steps):
            sum_ref[pl.ds(at[s], 8), :] = gather_sums(part_ref, s * 64, 8)
        return carry

    lax.fori_loop(0, reach // 8, functools.partial(block, units=True), 0)
    lax.fori_loop(reach // 8, rows // 8, functools.partial(block, units=False), 0)
    mixed_ref[...] = (sum_ref[...] + skip_ref[...] * values) * act_ref[...]

    copies[7].wait()
    prepare_scan(
        lengths_ref, proj_ref, prefill_x_ref, weight_ref, bias_ref, alog_ref, size_ref, force_ref,
        vec_ref, rates_ref,
    )
    scan(size_ref, force_ref, vec_ref, rates_ref, sum_ref, part_ref, None)
    copies[8].wait()
    mixed = sum_ref[...] + skip_ref[...] * prefill_x_ref[...].astype(jnp.float32)
    out_ref[...] = (mixed * silu(prefill_gate_ref[...].astype(jnp.float32))).astype(out_ref.dtype)


def pass_on_kernel(source_ref, *refs):
    for i, ref in enumerate(refs[:-1]):
        refs[-1][i] = ref[1]


def combine_kernel(source_ref, mixed_ref, unit_ref, swapped_ref, *rest):
    out_ref, recv_ref = rest[-2:]
    reach, steps = unit_ref.shape[:2]
    for i, ref in enumerate(rest[:-2]):
        recv_ref[2 * i * CAP : (2 * i + 1) * CAP] = ref[0]
        recv_ref[(2 * i + 1) * CAP : (2 * i + 2) * CAP] = swapped_ref[i]
    rows = mixed_ref.shape[0] // steps
    added = [[] for _ in range(steps)]
    for n in range(reach):
        source = source_ref[n]
        state = jnp.where(source >= 0, recv_ref[jnp.maximum(source, 0)], 0.0)
        for s in range(steps):
            added[s].append(jnp.sum(unit_ref[n, s] * state, axis=0, keepdims=True))
    for s in range(steps):
        first, last = s * rows, (s + 1) * rows
        out_ref[first : first + reach, :] = (
            mixed_ref[first : first + reach, :] + jnp.concatenate(added[s], axis=0)
        ).astype(out_ref.dtype)
        out_ref[first + reach : last, :] = mixed_ref[first + reach : last, :].astype(out_ref.dtype)


def local(
    prefill_x, prefill_gate, lengths, routes, decode_x, decode_gate, cached_state, xproj_weight,
    dt_weight, dt_bias, a_log, skip_gain, *, ranks, groups,
):
    tokens, channels = prefill_x.shape
    steps, rows, _ = decode_x.shape
    width = a_log.shape[0]
    requests = lengths.shape[1]
    columns = xproj_weight.shape[1]
    total = steps * rows
    reach = groups * CAP
    decode_flat = decode_x.reshape(total, channels)
    gate_flat = decode_gate.reshape(total, channels)
    bias = dt_bias.reshape(1, channels)
    skip = skip_gain.reshape(1, channels)
    rank = dt_weight.shape[0]
    height = 8 * (rank // LANES) + 2
    routes = routes.T
    flat = struct((ranks * height, LANES))

    def exchange(rows):
        chunks = rows.reshape(ranks, height // 2, 2, LANES)
        return lax.all_to_all(chunks, "tp", 0, 0).reshape(ranks * height, LANES)

    partial = call(
        functools.partial(project_kernel, rank=rank), "project", flat, [ANY] * 3,
        scratch=[
            bf16(columns, channels), bf16(tokens, channels), bf16(total, channels),
            pltpu.SemaphoreType.DMA((3,)),
        ],
    )(*stay(xproj_weight.T, prefill_x, decode_flat))
    copies = call(functools.partial(total_kernel, ranks=ranks), "total", flat, [VMEM])(
        exchange(partial)
    )
    proj = exchange(copies)

    scan_scratch = [
        f32(tokens, channels), f32(tokens, channels), f32(2 * width, tokens), f32(width, channels)
    ]
    chips = groups // 2
    send = call(
        states_kernel, "states", (struct((2, CAP, width, channels)),) * chips,
        [SMEM, SMEM] + [VMEM] * 5,
        out_specs=(VMEM,) * chips,
        scratch=scan_scratch
        + [f32(tokens, width, channels), f32(chips, 2, CAP, width, channels)],
    )(lengths, routes, proj, prefill_x, dt_weight, bias, a_log)

    def move(states, ahead, other):
        pairs = [
            (g, (g // 2 + ahead) % chips * 2 + (g + other) % 2) for g in range(groups)
        ]
        return lax.ppermute(states, "group", pairs)

    arrived = [send[0]] + [None] * (chips - 1)
    for ahead in sorted(range(1, chips), key=lambda d: min(d, chips - d)):
        arrived[ahead] = move(send[ahead], ahead, 0)
    prefill_out, mixed, unit, source = call(
        functools.partial(rest_kernel, groups=groups), "rest",
        (
            struct((tokens, channels), jnp.bfloat16), struct((total, channels)),
            struct((reach, steps, width, channels)), struct((reach,), jnp.int32),
        ),
        [SMEM, SMEM, VMEM] + [ANY] * 9,
        out_specs=(VMEM, VMEM, VMEM, SMEM),
        scratch=[
            f32(rows, width, channels), bf16(total, channels), bf16(total, channels),
            bf16(*dt_weight.shape), f32(width, channels), f32(1, channels), f32(1, channels),
            bf16(tokens, channels), bf16(tokens, channels),
            f32(total, channels), f32(total, channels), f32(total, channels),
            f32(total, channels), f32(channels // LANES, steps * 64, LANES), f32(2 * width, total),
            f32(width, channels), pltpu.SemaphoreType.DMA((9,)),
        ],
        flops=8 * 10**9,
    )(
        lengths, routes, proj,
        *stay(
            cached_state, decode_flat, gate_flat, dt_weight, a_log, bias, skip, prefill_x,
            prefill_gate,
        ),
    )
    swapped = move(
        call(
            pass_on_kernel, "pass_on", struct((chips, CAP, width, channels)),
            [SMEM] + [VMEM] * chips,
        )(source, *arrived),
        0, 1,
    )
    decode_out = call(
        combine_kernel, "combine", struct((total, channels), jnp.bfloat16),
        [SMEM] + [VMEM] * (3 + chips),
        scratch=[f32(reach, width, channels)],
    )(source, mixed, unit, swapped, *arrived)
    return prefill_out, decode_out.reshape(steps, rows, channels)


def solution(mesh):
    placed = (
        P("group", "tp"), P("group", "tp"), P("group", None), P(), P(None, "group", "tp"),
        P(None, "group", "tp"), P("group", None, "tp"), P("tp", None), P(None, "tp"), P("tp"),
        P(None, "tp"), P("tp"),
    )
    body = functools.partial(local, ranks=mesh.shape["tp"], groups=mesh.shape["group"])
    return jax.shard_map(
        body, mesh=mesh, in_specs=placed, out_specs=(P("group", "tp"), P(None, "group", "tp")),
        check_vma=False,
    )
```

```python
import functools

import jax
import jax.numpy as jnp
from jax import lax
from jax.experimental import pallas as pl
from jax.experimental.pallas import tpu as pltpu
from jax.sharding import PartitionSpec as P

LOG2E = 1.4426950408889634
FAR = 1e30
LANES = 128
CAP = 2

VMEM = pl.BlockSpec(memory_space=pltpu.VMEM)
SMEM = pl.BlockSpec(memory_space=pltpu.SMEM)
ANY = pl.BlockSpec(memory_space=pl.ANY)


def call(kernel, name, out_shape, in_specs, out_specs=VMEM, scratch=(), mib=16, flops=0):
    return pl.pallas_call(
        kernel,
        grid=(1,),
        out_shape=out_shape,
        in_specs=in_specs,
        out_specs=out_specs,
        scratch_shapes=scratch,
        compiler_params=pltpu.CompilerParams(vmem_limit_bytes=mib << 20),
        cost_estimate=pl.CostEstimate(flops=flops, bytes_accessed=1 << 20, transcendentals=0),
        name=name,
    )


def f32(*shape):
    return pltpu.VMEM(shape, jnp.float32)


def bf16(*shape):
    return pltpu.VMEM(shape, jnp.bfloat16)


def struct(shape, dtype=jnp.float32):
    return jax.ShapeDtypeStruct(shape, dtype)


def stay(*arrays):
    return tuple(pltpu.with_memory_space_constraint(a, pltpu.HBM) for a in arrays)


def fetch(sources, targets, sems):
    copies = [
        pltpu.make_async_copy(a, b, sems.at[i]) for i, (a, b) in enumerate(zip(sources, targets))
    ]
    for copy in copies:
        copy.start()
    return copies


def softplus(v):
    return jnp.maximum(v, 0.0) + jnp.log1p(jnp.exp(-jnp.abs(v)))


def silu(v):
    return v / (1.0 + jnp.exp(-v))


def tiles_of(channels):
    return [slice(t, t + LANES) for t in range(0, channels, LANES)]


def low_rows(rank, j, tile):
    first = j * (8 * (rank // LANES) + 2) + 8 * tile
    return slice(first, first + 8)


def vector_rows(rank, count, which):
    height = 8 * (rank // LANES) + 2
    return pl.ds(height - 2 + which, count, stride=height)


def low_part(proj_ref, rank, half, which):
    tiles = range(rank // LANES)
    return jnp.concatenate(
        [
            jnp.concatenate([proj_ref[low_rows(rank, j, tile), :] for tile in tiles], axis=1)
            for j in range(half * which, half * (which + 1))
        ],
        axis=0,
    )


def project_kernel(
    weight_hbm, prefill_hbm, decode_hbm, out_ref, weight_ref, prefill_ref, decode_ref, sems,
    *, rank,
):
    copies = fetch(
        (weight_hbm, prefill_hbm, decode_hbm), (weight_ref, prefill_ref, decode_ref), sems
    )
    count = weight_ref.shape[0] - rank
    for copy in copies:
        copy.wait()
    values = jnp.concatenate([prefill_ref[...], decode_ref[...]], axis=0)
    low = lax.dot_general(
        values, weight_ref[:rank], (((1,), (1,)), ((), ())), preferred_element_type=jnp.float32
    )
    for j in range(count):
        for tile, cols in enumerate(tiles_of(rank)):
            out_ref[low_rows(rank, j, tile), :] = low[8 * j : 8 * j + 8, cols]
    vectors = lax.dot_general(
        weight_ref[rank:], values, (((1,), (1,)), ((), ())), preferred_element_type=jnp.float32
    )
    rows = prefill_ref.shape[0]
    for which in range(2):
        out_ref[vector_rows(rank, count, which), :] = vectors[:, which * rows : (which + 1) * rows]


def total_kernel(parts_ref, out_ref, *, ranks):
    height = parts_ref.shape[0] // ranks
    group = 4
    quad = parts_ref[...].reshape(ranks // group, group * height, LANES).sum(axis=0)
    total = quad[:height]
    for i in range(1, group):
        total = total + quad[i * height : (i + 1) * height]
    quad = jnp.concatenate([total] * group, axis=0)
    for i in range(ranks // group):
        out_ref[i * group * height : (i + 1) * group * height, :] = quad


def step_sizes(low, weight_ref, bias_ref):
    low = low.astype(jnp.bfloat16)
    return softplus(
        jnp.dot(low, weight_ref[...], preferred_element_type=jnp.float32) + bias_ref[...]
    )


def fold(terms):
    return sum(terms[i : i + 8] for i in range(8, terms.shape[0], 8)) + terms[:8]


def gather_sums(part_ref, first, stride):
    return jnp.concatenate(
        [
            sum(
                (part_ref[tile, pl.ds(first + j, 8, stride=stride), :] for j in range(1, 8)),
                part_ref[tile, pl.ds(first, 8, stride=stride), :],
            )
            for tile in range(part_ref.shape[0])
        ],
        axis=1,
    )


def advance(hidden, rates_ref, size_row, forcing_row, inject, readout, part_ref, at):
    for tile, cols in enumerate(tiles_of(size_row.shape[1])):
        damping = jnp.exp2(size_row[:, cols] * rates_ref[:, cols])
        hidden[tile] = damping * hidden[tile] + forcing_row[:, cols] * inject
        if readout is not None:
            part_ref[tile, at : at + 8, :] = fold(readout * hidden[tile])


def prepare_scan(table, lengths_ref, proj_ref, x_ref, weight_ref, bias_ref, alog_ref, size_ref, force_ref, vec_ref, rates_ref):
    tokens, channels = x_ref.shape
    rank = weight_ref.shape[0]
    count = vec_ref.shape[0]
    low = low_part(proj_ref, rank, count // 2, 0)
    size = step_sizes(low, weight_ref, bias_ref)
    force_ref[...] = size * x_ref[...].astype(jnp.float32)
    vec_ref[...] = proj_ref[vector_rows(rank, count, 0), :]
    rates_ref[...] = -LOG2E * jnp.exp(alog_ref[...])
    table.wait()
    position = lax.broadcasted_iota(jnp.int32, (tokens, LANES), 0)
    first = position == 0
    begin = jnp.int32(0)
    ends = []
    for k in range(lengths_ref.shape[1]):
        first = first | (position == begin)
        begin = begin + lengths_ref[0, k]
        ends.append(begin - 1)
    reset = jnp.where(first, jnp.float32(FAR), jnp.float32(0.0))
    for cols in tiles_of(channels):
        size_ref[:, cols] = size[:, cols] + reset
    return ends


def scan(size_ref, force_ref, vec_ref, rates_ref, mixed_ref, part_ref, hist_ref):
    tokens, channels = size_ref.shape
    width = rates_ref.shape[0]
    tiles = tiles_of(channels)

    def block(b, hidden):
        base = pl.multiple_of(b * 8, 8)
        vectors = pltpu.roll(vec_ref[...], tokens - base, axis=1)
        sizes = size_ref[pl.ds(base, 8), :]
        forces = force_ref[pl.ds(base, 8), :]
        hidden = list(hidden)
        for i in range(8):
            inject = jnp.broadcast_to(vectors[:width, i : i + 1], (width, LANES))
            readout = None
            if mixed_ref is not None:
                readout = jnp.broadcast_to(vectors[width:, i : i + 1], (width, LANES))
            advance(
                hidden, rates_ref, sizes[i : i + 1], forces[i : i + 1], inject, readout,
                part_ref, i * 8,
            )
            if hist_ref is not None:
                for tile, cols in enumerate(tiles):
                    hist_ref[base + i, :, cols] = hidden[tile]
        if mixed_ref is not None:
            mixed_ref[pl.ds(base, 8), :] = gather_sums(part_ref, 0, 8)
        return tuple(hidden)

    zero = jnp.zeros((width, LANES), jnp.float32)
    lax.fori_loop(0, tokens // 8, block, (zero,) * len(tiles), unroll=16)


def states_kernel(
    lengths_any, routes_any, proj_ref, x_ref, weight_ref, bias_ref, alog_ref,
    *rest,
):
    send_refs, rest = rest[:-9], rest[-9:]
    lengths_ref, routes_ref, size_ref, force_ref, vec_ref, rates_ref, hist_ref, send_ref, sems = rest
    tables = fetch((lengths_any, routes_any), (lengths_ref, routes_ref), sems)
    chips = len(send_refs)
    requests = lengths_ref.shape[1]
    group = lax.axis_index("group")
    ends = prepare_scan(
        tables[0], lengths_ref, proj_ref, x_ref, weight_ref, bias_ref, alog_ref, size_ref, force_ref, vec_ref,
        rates_ref,
    )
    scan(size_ref, force_ref, vec_ref, rates_ref, None, None, hist_ref)
    tables[1].wait()
    dests = [routes_ref[0, group * requests + k] for k in range(requests)]
    for k in range(requests):
        lane = jnp.int32(0)
        for j in range(k):
            lane = lane + (dests[j] == dests[k]).astype(jnp.int32)
        ahead = lax.rem(dests[k] // 2 - group // 2 + chips, chips)
        other = lax.rem(dests[k] + group, 2)
        send_ref[ahead, other, lane] = hist_ref[ends[k]]
    for chip in range(chips):
        send_refs[chip][...] = send_ref[chip]


def rest_kernel(
    proj_ref, weight_ref, alog_ref, bias_ref, prefill_x_ref,
    lengths_any, routes_any, prefill_gate_hbm, skip_hbm, decode_x_hbm, decode_gate_hbm, state_hbm,
    out_ref, mixed_ref, unit_ref, row_ref,
    lengths_ref, routes_ref, prefill_gate_ref, skip_ref, decode_x_ref, decode_gate_ref, state_ref,
    source_ref, size_ref, force_ref, act_ref, sum_ref, part_ref, vec_ref, rates_ref, sems, *, groups,
):
    copies = fetch(
        (
            lengths_any, routes_any, prefill_gate_hbm, skip_hbm, decode_x_hbm, decode_gate_hbm,
            state_hbm,
        ),
        (
            lengths_ref, routes_ref, prefill_gate_ref, skip_ref, decode_x_ref, decode_gate_ref,
            state_ref,
        ),
        sems,
    )
    total, channels = decode_x_ref.shape
    rows, width = state_ref.shape[:2]
    steps = total // rows
    reach = source_ref.shape[0]
    tiles = tiles_of(channels)
    rank = weight_ref.shape[0]
    count = vec_ref.shape[0]
    requests = lengths_ref.shape[1]
    me = lax.axis_index("group")

    prepare_scan(
        copies[0], lengths_ref, proj_ref, prefill_x_ref, weight_ref, bias_ref, alog_ref, size_ref,
        force_ref, vec_ref, rates_ref,
    )
    scan(size_ref, force_ref, vec_ref, rates_ref, sum_ref, part_ref, None)
    copies[2].wait()
    copies[3].wait()
    mixed = sum_ref[...] + skip_ref[...] * prefill_x_ref[...].astype(jnp.float32)
    out_ref[...] = (mixed * silu(prefill_gate_ref[...].astype(jnp.float32))).astype(out_ref.dtype)

    copies[1].wait()
    for n in range(reach):
        source_ref[n] = reach
        row_ref[n] = -1
    slot = jnp.int32(0)
    for g in range(groups):
        lane = jnp.int32(0)
        for k in range(requests):
            ours = routes_ref[0, g * requests + k] == me

            @pl.when(ours)
            def _(g=g, slot=slot, lane=lane):
                behind = lax.rem(me // 2 - g // 2 + groups // 2, groups // 2)
                source = (behind * 2 + lax.rem(me + g, 2)) * CAP + lane
                source_ref[slot] = source
                row_ref[source] = slot

            slot = slot + ours.astype(jnp.int32)
            lane = lane + ours.astype(jnp.int32)

    copies[4].wait()
    copies[5].wait()
    size = step_sizes(low_part(proj_ref, rank, count // 2, 1), weight_ref, bias_ref)
    values = decode_x_ref[...].astype(jnp.float32)
    size_ref[...] = size
    force_ref[...] = size * values
    vec_ref[...] = proj_ref[vector_rows(rank, count, 1), :]
    act_ref[...] = silu(decode_gate_ref[...].astype(jnp.float32))
    copies[6].wait()

    def block(b, carry, units):
        base = pl.multiple_of(b * 8, 8)
        at = [pl.multiple_of(s * rows + base, 8) for s in range(steps)]
        vectors = [pltpu.roll(vec_ref[...], total - at[s], axis=1) for s in range(steps)]
        sizes = [size_ref[pl.ds(at[s], 8), :] for s in range(steps)]
        forces = [force_ref[pl.ds(at[s], 8), :] for s in range(steps)]
        acts = [act_ref[pl.ds(at[s], 8), :] for s in range(steps)]
        for i in range(8):
            hidden = [state_ref[base + i, :, cols] for cols in tiles]
            if units:
                source = source_ref[base + i]
                hidden = [jnp.where(source < reach, 0.0, start) for start in hidden]
            summed = None
            for s in range(steps):
                inject = jnp.broadcast_to(vectors[s][:width, i : i + 1], (width, LANES))
                readout = jnp.broadcast_to(vectors[s][width:, i : i + 1], (width, LANES))
                row = sizes[s][i : i + 1]
                advance(
                    hidden, rates_ref, row, forces[s][i : i + 1], inject, readout, part_ref,
                    (s * 8 + i) * 8,
                )
                if units:
                    summed = row if s == 0 else summed + row
                    for cols in tiles:
                        unit_ref[source, s, :, cols] = (
                            readout * acts[s][i : i + 1, cols]
                        ) * jnp.exp2(summed[:, cols] * rates_ref[:, cols])
        for s in range(steps):
            sum_ref[pl.ds(at[s], 8), :] = gather_sums(part_ref, s * 64, 8)
        return carry

    lax.fori_loop(0, reach // 8, functools.partial(block, units=True), 0)
    lax.fori_loop(reach // 8, rows // 8, functools.partial(block, units=False), 0)
    mixed_ref[...] = (sum_ref[...] + skip_ref[...] * values) * act_ref[...]


def pass_on_kernel(mixed_ref, *refs):
    for i, ref in enumerate(refs[:-1]):
        refs[-1][i] = ref[1]


def combine_kernel(row_any, mixed_ref, unit_ref, swapped_ref, *rest):
    here_refs, (out_ref, row_ref, sum_ref, sems) = rest[:-4], rest[-4:]
    (table,) = fetch((row_any,), (row_ref,), sems)
    steps = unit_ref.shape[1]
    rows = mixed_ref.shape[0] // steps
    sum_ref[...] = mixed_ref[...]
    added = []
    for i, ref in enumerate(here_refs):
        for c in range(2 * CAP):
            state = ref[0, c] if c < CAP else swapped_ref[i, c - CAP]
            for s in range(steps):
                terms = unit_ref[2 * CAP * i + c, s] * state
                added.append(jnp.sum(terms, axis=0, keepdims=True))
    table.wait()
    for i, term in enumerate(added):
        row = row_ref[i // steps]
        at = pl.ds(i % steps * rows + jnp.maximum(row, 0), 1)
        sum_ref[at, :] = sum_ref[at, :] + jnp.where(row >= 0, term, 0.0)
    out_ref[...] = sum_ref[...].astype(out_ref.dtype)


def local(
    prefill_x, prefill_gate, lengths, routes, decode_x, decode_gate, cached_state, xproj_weight,
    dt_weight, dt_bias, a_log, skip_gain, *, ranks, groups,
):
    tokens, channels = prefill_x.shape
    steps, rows, _ = decode_x.shape
    width = a_log.shape[0]
    requests = lengths.shape[1]
    columns = xproj_weight.shape[1]
    total = steps * rows
    reach = groups * CAP
    decode_flat = decode_x.reshape(total, channels)
    gate_flat = decode_gate.reshape(total, channels)
    bias = dt_bias.reshape(1, channels)
    skip = skip_gain.reshape(1, channels)
    rank = dt_weight.shape[0]
    height = 8 * (rank // LANES) + 2
    routes = routes.T
    flat = struct((ranks * height, LANES))

    def exchange(rows):
        chunks = rows.reshape(ranks, height // 2, 2, LANES)
        return lax.all_to_all(chunks, "tp", 0, 0).reshape(ranks * height, LANES)

    partial = call(
        functools.partial(project_kernel, rank=rank), "project", flat, [ANY] * 3,
        scratch=[
            bf16(columns, channels), bf16(tokens, channels), bf16(total, channels),
            pltpu.SemaphoreType.DMA((3,)),
        ],
    )(*stay(xproj_weight.T, prefill_x, decode_flat))
    copies = call(functools.partial(total_kernel, ranks=ranks), "total", flat, [VMEM])(
        exchange(partial)
    )
    proj = exchange(copies)

    tables = [pltpu.SMEM(lengths.shape, jnp.int32), pltpu.SMEM(routes.shape, jnp.int32)]
    scan_scratch = [
        f32(tokens, channels), f32(tokens, channels), f32(2 * width, tokens), f32(width, channels)
    ]
    chips = groups // 2
    send = call(
        states_kernel, "states", (struct((2, CAP, width, channels)),) * chips,
        [ANY, ANY] + [VMEM] * 5,
        out_specs=(VMEM,) * chips,
        scratch=tables + scan_scratch
        + [
            f32(tokens, width, channels), f32(chips, 2, CAP, width, channels),
            pltpu.SemaphoreType.DMA((2,)),
        ],
    )(lengths, routes, proj, prefill_x, dt_weight, bias, a_log)

    def move(states, ahead, other):
        pairs = [
            (g, (g // 2 + ahead) % chips * 2 + (g + other) % 2) for g in range(groups)
        ]
        return lax.ppermute(states, "group", pairs)

    arrived = [send[0]] + [None] * (chips - 1)
    for ahead in sorted(range(1, chips), key=lambda d: min(d, chips - d)):
        arrived[ahead] = move(send[ahead], ahead, 0)
    prefill_out, mixed, unit, row_of = call(
        functools.partial(rest_kernel, groups=groups), "rest",
        (
            struct((tokens, channels), jnp.bfloat16), struct((total, channels)),
            struct((reach + 1, steps, width, channels)), struct((reach,), jnp.int32),
        ),
        [VMEM] * 5 + [ANY] * 7,
        out_specs=(VMEM, VMEM, VMEM, SMEM),
        scratch=tables + [
            bf16(tokens, channels), f32(1, channels), bf16(total, channels),
            bf16(total, channels), f32(rows, width, channels),
            pltpu.SMEM((reach,), jnp.int32),
            f32(total, channels), f32(total, channels), f32(total, channels),
            f32(total, channels), f32(channels // LANES, steps * 64, LANES),
            f32(2 * width, total), f32(width, channels), pltpu.SemaphoreType.DMA((7,)),
        ],
        flops=8 * 10**9,
    )(
        proj, dt_weight, a_log, bias, prefill_x, lengths, routes,
        *stay(prefill_gate, skip, decode_flat, gate_flat, cached_state),
    )
    swapped = move(
        call(
            pass_on_kernel, "pass_on", struct((chips, CAP, width, channels)),
            [ANY] + [VMEM] * chips,
        )(mixed, *arrived),
        0, 1,
    )
    decode_out = call(
        combine_kernel, "combine", struct((total, channels), jnp.bfloat16),
        [ANY] + [VMEM] * (3 + chips),
        scratch=[
            pltpu.SMEM((reach,), jnp.int32), f32(total, channels), pltpu.SemaphoreType.DMA((1,)),
        ],
    )(row_of, mixed, unit, swapped, *arrived)
    return prefill_out, decode_out.reshape(steps, rows, channels)


def solution(mesh):
    placed = (
        P("group", "tp"), P("group", "tp"), P("group", None), P(), P(None, "group", "tp"),
        P(None, "group", "tp"), P("group", None, "tp"), P("tp", None), P(None, "tp"), P("tp"),
        P(None, "tp"), P("tp"),
    )
    body = functools.partial(local, ranks=mesh.shape["tp"], groups=mesh.shape["group"])
    return jax.shard_map(
        body, mesh=mesh, in_specs=placed, out_specs=(P("group", "tp"), P(None, "group", "tp")),
        check_vma=False,
    )
```

```python
import functools

import jax
import jax.numpy as jnp
from jax import lax
from jax.experimental import pallas as pl
from jax.experimental.pallas import tpu as pltpu
from jax.sharding import PartitionSpec as P

LOG2E = 1.4426950408889634
FAR = 1e30
LANES = 128
CAP = 2

VMEM = pl.BlockSpec(memory_space=pltpu.VMEM)
SMEM = pl.BlockSpec(memory_space=pltpu.SMEM)
ANY = pl.BlockSpec(memory_space=pl.ANY)


def call(kernel, name, out_shape, in_specs, out_specs=VMEM, scratch=(), mib=16, flops=0):
    return pl.pallas_call(
        kernel,
        grid=(1,),
        out_shape=out_shape,
        in_specs=in_specs,
        out_specs=out_specs,
        scratch_shapes=scratch,
        compiler_params=pltpu.CompilerParams(vmem_limit_bytes=mib << 20),
        cost_estimate=pl.CostEstimate(flops=flops, bytes_accessed=1 << 20, transcendentals=0),
        name=name,
    )


def f32(*shape):
    return pltpu.VMEM(shape, jnp.float32)


def bf16(*shape):
    return pltpu.VMEM(shape, jnp.bfloat16)


def struct(shape, dtype=jnp.float32):
    return jax.ShapeDtypeStruct(shape, dtype)


def stay(*arrays):
    return tuple(pltpu.with_memory_space_constraint(a, pltpu.HBM) for a in arrays)


def fetch(sources, targets, sems):
    copies = [
        pltpu.make_async_copy(a, b, sems.at[i]) for i, (a, b) in enumerate(zip(sources, targets))
    ]
    for copy in copies:
        copy.start()
    return copies


def softplus(v):
    return jnp.maximum(v, 0.0) + jnp.log1p(jnp.exp(-jnp.abs(v)))


def silu(v):
    return v / (1.0 + jnp.exp(-v))


def tiles_of(channels):
    return [slice(t, t + LANES) for t in range(0, channels, LANES)]


def low_rows(rank, j, tile):
    first = j * (8 * (rank // LANES) + 2) + 8 * tile
    return slice(first, first + 8)


def vector_rows(rank, count, which):
    height = 8 * (rank // LANES) + 2
    return pl.ds(height - 2 + which, count, stride=height)


def low_part(proj_ref, rank, half, which):
    tiles = range(rank // LANES)
    return jnp.concatenate(
        [
            jnp.concatenate([proj_ref[low_rows(rank, j, tile), :] for tile in tiles], axis=1)
            for j in range(half * which, half * (which + 1))
        ],
        axis=0,
    )


def project_kernel(
    weight_hbm, prefill_hbm, decode_hbm, out_ref, weight_ref, prefill_ref, decode_ref, sems,
    *, rank,
):
    copies = fetch(
        (weight_hbm, prefill_hbm, decode_hbm), (weight_ref, prefill_ref, decode_ref), sems
    )
    count = weight_ref.shape[0] - rank
    for copy in copies:
        copy.wait()
    values = jnp.concatenate([prefill_ref[...], decode_ref[...]], axis=0)
    low = lax.dot_general(
        values, weight_ref[:rank], (((1,), (1,)), ((), ())), preferred_element_type=jnp.float32
    )
    for j in range(count):
        for tile, cols in enumerate(tiles_of(rank)):
            out_ref[low_rows(rank, j, tile), :] = low[8 * j : 8 * j + 8, cols]
    vectors = lax.dot_general(
        weight_ref[rank:], values, (((1,), (1,)), ((), ())), preferred_element_type=jnp.float32
    )
    rows = prefill_ref.shape[0]
    for which in range(2):
        out_ref[vector_rows(rank, count, which), :] = vectors[:, which * rows : (which + 1) * rows]


def total_kernel(parts_ref, out_ref, *, ranks):
    height = parts_ref.shape[0] // ranks
    group = 4
    quad = parts_ref[...].reshape(ranks // group, group * height, LANES).sum(axis=0)
    total = quad[:height]
    for i in range(1, group):
        total = total + quad[i * height : (i + 1) * height]
    quad = jnp.concatenate([total] * group, axis=0)
    for i in range(ranks // group):
        out_ref[i * group * height : (i + 1) * group * height, :] = quad


def step_sizes(low, weight_ref, bias_ref):
    low = low.astype(jnp.bfloat16)
    return softplus(
        jnp.dot(low, weight_ref[...], preferred_element_type=jnp.float32) + bias_ref[...]
    )


def fold(terms):
    return sum(terms[i : i + 8] for i in range(8, terms.shape[0], 8)) + terms[:8]


def gather_sums(part_ref, first, stride):
    return jnp.concatenate(
        [
            sum(
                (part_ref[tile, pl.ds(first + j, 8, stride=stride), :] for j in range(1, 8)),
                part_ref[tile, pl.ds(first, 8, stride=stride), :],
            )
            for tile in range(part_ref.shape[0])
        ],
        axis=1,
    )


def advance(hidden, rates_ref, size_row, forcing_row, inject, readout, part_ref, at):
    for tile, cols in enumerate(tiles_of(size_row.shape[1])):
        damping = jnp.exp2(size_row[:, cols] * rates_ref[:, cols])
        hidden[tile] = damping * hidden[tile] + forcing_row[:, cols] * inject
        if readout is not None:
            part_ref[tile, at : at + 8, :] = fold(readout * hidden[tile])


def prepare_scan(table, lengths_ref, proj_ref, x_ref, weight_ref, bias_ref, alog_ref, size_ref, force_ref, vec_ref, rates_ref):
    tokens, channels = x_ref.shape
    rank = weight_ref.shape[0]
    count = vec_ref.shape[0]
    low = low_part(proj_ref, rank, count // 2, 0)
    size = step_sizes(low, weight_ref, bias_ref)
    force_ref[...] = size * x_ref[...].astype(jnp.float32)
    vec_ref[...] = proj_ref[vector_rows(rank, count, 0), :]
    rates_ref[...] = -LOG2E * jnp.exp(alog_ref[...])
    table.wait()
    position = lax.broadcasted_iota(jnp.int32, (tokens, LANES), 0)
    first = position == 0
    begin = jnp.int32(0)
    ends = []
    for k in range(lengths_ref.shape[1]):
        first = first | (position == begin)
        begin = begin + lengths_ref[0, k]
        ends.append(begin - 1)
    reset = jnp.where(first, jnp.float32(FAR), jnp.float32(0.0))
    for cols in tiles_of(channels):
        size_ref[:, cols] = size[:, cols] + reset
    return ends


def scan(size_ref, force_ref, vec_ref, rates_ref, mixed_ref, part_ref, hist_ref):
    tokens, channels = size_ref.shape
    width = rates_ref.shape[0]
    tiles = tiles_of(channels)

    def block(b, hidden):
        base = pl.multiple_of(b * 8, 8)
        vectors = pltpu.roll(vec_ref[...], tokens - base, axis=1)
        sizes = size_ref[pl.ds(base, 8), :]
        forces = force_ref[pl.ds(base, 8), :]
        hidden = list(hidden)
        for i in range(8):
            inject = jnp.broadcast_to(vectors[:width, i : i + 1], (width, LANES))
            readout = None
            if mixed_ref is not None:
                readout = jnp.broadcast_to(vectors[width:, i : i + 1], (width, LANES))
            advance(
                hidden, rates_ref, sizes[i : i + 1], forces[i : i + 1], inject, readout,
                part_ref, i * 8,
            )
            if hist_ref is not None:
                for tile, cols in enumerate(tiles):
                    hist_ref[base + i, :, cols] = hidden[tile]
        if mixed_ref is not None:
            mixed_ref[pl.ds(base, 8), :] = gather_sums(part_ref, 0, 8)
        return tuple(hidden)

    zero = jnp.zeros((width, LANES), jnp.float32)
    lax.fori_loop(0, tokens // 8, block, (zero,) * len(tiles), unroll=16)


def places_on(source, dest, chips):
    on = dest // 2 - source // 2 + chips
    return lax.rem(jnp.where(lax.rem(source, 2) == 0, on, 2 * chips - on), chips)


def far_first(chips):
    return sorted(range(chips), key=lambda ahead: -min(ahead, chips - ahead))


def states_kernel(
    lengths_any, routes_any, proj_ref, x_ref, weight_ref, bias_ref, alog_ref,
    *rest,
):
    size_ref, force_ref, *send_refs = rest[:-7]
    lengths_ref, routes_ref, vec_ref, rates_ref, hist_ref, send_ref, sems = rest[-7:]
    tables = fetch((lengths_any, routes_any), (lengths_ref, routes_ref), sems)
    chips = len(send_refs)
    requests = lengths_ref.shape[1]
    group = lax.axis_index("group")
    ends = prepare_scan(
        tables[0], lengths_ref, proj_ref, x_ref, weight_ref, bias_ref, alog_ref, size_ref, force_ref, vec_ref,
        rates_ref,
    )
    scan(size_ref, force_ref, vec_ref, rates_ref, None, None, hist_ref)
    tables[1].wait()
    dests = [routes_ref[0, group * requests + k] for k in range(requests)]
    for k in range(requests):
        lane = jnp.int32(0)
        for j in range(k):
            lane = lane + (dests[j] == dests[k]).astype(jnp.int32)
        ahead = places_on(group, dests[k], chips)
        other = lax.rem(dests[k] + group, 2)
        send_ref[ahead, other, lane] = hist_ref[ends[k]]
    for ref, ahead in zip(send_refs, far_first(chips)):
        ref[...] = send_ref[ahead]


def rest_kernel(
    proj_ref, weight_ref, alog_ref, bias_ref, prefill_x_ref,
    prefill_size_ref, prefill_force_ref,
    routes_any, prefill_gate_hbm, skip_hbm, decode_x_hbm, decode_gate_hbm, state_hbm,
    out_ref, mixed_ref, unit_ref, row_ref,
    routes_ref, prefill_gate_ref, skip_ref, decode_x_ref, decode_gate_ref, state_ref,
    source_ref, size_ref, force_ref, act_ref, sum_ref, part_ref, vec_ref, rates_ref, sems, *, groups,
):
    copies = fetch(
        (routes_any, prefill_gate_hbm, skip_hbm, decode_x_hbm, decode_gate_hbm, state_hbm),
        (routes_ref, prefill_gate_ref, skip_ref, decode_x_ref, decode_gate_ref, state_ref),
        sems,
    )
    total, channels = decode_x_ref.shape
    rows, width = state_ref.shape[:2]
    steps = total // rows
    reach = source_ref.shape[0]
    tiles = tiles_of(channels)
    rank = weight_ref.shape[0]
    count = vec_ref.shape[0]
    requests = routes_ref.shape[1] // groups
    me = lax.axis_index("group")

    rates_ref[...] = -LOG2E * jnp.exp(alog_ref[...])
    vec_ref[...] = proj_ref[vector_rows(rank, count, 0), :]
    scan(prefill_size_ref, prefill_force_ref, vec_ref, rates_ref, sum_ref, part_ref, None)
    copies[1].wait()
    copies[2].wait()
    mixed = sum_ref[...] + skip_ref[...] * prefill_x_ref[...].astype(jnp.float32)
    out_ref[...] = (mixed * silu(prefill_gate_ref[...].astype(jnp.float32))).astype(out_ref.dtype)

    copies[0].wait()
    for n in range(reach):
        source_ref[n] = reach
        row_ref[n] = -1
    slot = jnp.int32(0)
    for g in range(groups):
        lane = jnp.int32(0)
        for k in range(requests):
            ours = routes_ref[0, g * requests + k] == me

            @pl.when(ours)
            def _(g=g, slot=slot, lane=lane):
                behind = places_on(jnp.int32(g), me, groups // 2)
                source = (behind * 2 + lax.rem(me + g, 2)) * CAP + lane
                source_ref[slot] = source
                row_ref[source] = slot

            slot = slot + ours.astype(jnp.int32)
            lane = lane + ours.astype(jnp.int32)

    copies[3].wait()
    copies[4].wait()
    size = step_sizes(low_part(proj_ref, rank, count // 2, 1), weight_ref, bias_ref)
    values = decode_x_ref[...].astype(jnp.float32)
    size_ref[...] = size
    force_ref[...] = size * values
    vec_ref[...] = proj_ref[vector_rows(rank, count, 1), :]
    act_ref[...] = silu(decode_gate_ref[...].astype(jnp.float32))
    copies[5].wait()

    def block(b, carry, units):
        base = pl.multiple_of(b * 8, 8)
        at = [pl.multiple_of(s * rows + base, 8) for s in range(steps)]
        vectors = [pltpu.roll(vec_ref[...], total - at[s], axis=1) for s in range(steps)]
        sizes = [size_ref[pl.ds(at[s], 8), :] for s in range(steps)]
        forces = [force_ref[pl.ds(at[s], 8), :] for s in range(steps)]
        acts = [act_ref[pl.ds(at[s], 8), :] for s in range(steps)]
        for i in range(8):
            hidden = [state_ref[base + i, :, cols] for cols in tiles]
            if units:
                source = source_ref[base + i]
                hidden = [jnp.where(source < reach, 0.0, start) for start in hidden]
            summed = None
            for s in range(steps):
                inject = jnp.broadcast_to(vectors[s][:width, i : i + 1], (width, LANES))
                readout = jnp.broadcast_to(vectors[s][width:, i : i + 1], (width, LANES))
                row = sizes[s][i : i + 1]
                advance(
                    hidden, rates_ref, row, forces[s][i : i + 1], inject, readout, part_ref,
                    (s * 8 + i) * 8,
                )
                if units:
                    summed = row if s == 0 else summed + row
                    for cols in tiles:
                        unit_ref[source, s, :, cols] = (
                            readout * acts[s][i : i + 1, cols]
                        ) * jnp.exp2(summed[:, cols] * rates_ref[:, cols])
        for s in range(steps):
            sum_ref[pl.ds(at[s], 8), :] = gather_sums(part_ref, s * 64, 8)
        return carry

    lax.fori_loop(0, reach // 8, functools.partial(block, units=True), 0)
    lax.fori_loop(reach // 8, rows // 8, functools.partial(block, units=False), 0)
    mixed_ref[...] = (sum_ref[...] + skip_ref[...] * values) * act_ref[...]


def pass_on_kernel(mixed_ref, *refs):
    for ref, ahead in zip(refs[:-1], far_first(len(refs) - 1)):
        refs[-1][ahead] = ref[1]


def combine_kernel(row_any, mixed_ref, unit_ref, swapped_ref, *rest):
    here_refs, (out_ref, row_ref, sum_ref, sems) = rest[:-4], rest[-4:]
    (table,) = fetch((row_any,), (row_ref,), sems)
    steps = unit_ref.shape[1]
    rows = mixed_ref.shape[0] // steps
    sum_ref[...] = mixed_ref[...]
    added = []
    for ref, ahead in zip(here_refs, far_first(len(here_refs))):
        for c in range(2 * CAP):
            state = ref[0, c] if c < CAP else swapped_ref[ahead, c - CAP]
            for s in range(steps):
                terms = unit_ref[2 * CAP * ahead + c, s] * state
                term = jnp.sum(terms, axis=0, keepdims=True)
                added.append((2 * CAP * ahead + c, s, term))
    table.wait()
    for slot, s, term in added:
        row = row_ref[slot]
        at = pl.ds(s * rows + jnp.maximum(row, 0), 1)
        sum_ref[at, :] = sum_ref[at, :] + jnp.where(row >= 0, term, 0.0)
    out_ref[...] = sum_ref[...].astype(out_ref.dtype)


def local(
    prefill_x, prefill_gate, lengths, routes, decode_x, decode_gate, cached_state, xproj_weight,
    dt_weight, dt_bias, a_log, skip_gain, *, ranks, groups,
):
    tokens, channels = prefill_x.shape
    steps, rows, _ = decode_x.shape
    width = a_log.shape[0]
    requests = lengths.shape[1]
    columns = xproj_weight.shape[1]
    total = steps * rows
    reach = groups * CAP
    decode_flat = decode_x.reshape(total, channels)
    gate_flat = decode_gate.reshape(total, channels)
    bias = dt_bias.reshape(1, channels)
    skip = skip_gain.reshape(1, channels)
    rank = dt_weight.shape[0]
    height = 8 * (rank // LANES) + 2
    routes = routes.T
    flat = struct((ranks * height, LANES))

    def exchange(rows):
        chunks = rows.reshape(ranks, height // 2, 2, LANES)
        return lax.all_to_all(chunks, "tp", 0, 0).reshape(ranks * height, LANES)

    partial = call(
        functools.partial(project_kernel, rank=rank), "project", flat, [ANY] * 3,
        scratch=[
            bf16(columns, channels), bf16(tokens, channels), bf16(total, channels),
            pltpu.SemaphoreType.DMA((3,)),
        ],
    )(*stay(xproj_weight.T, prefill_x, decode_flat))
    copies = call(functools.partial(total_kernel, ranks=ranks), "total", flat, [VMEM])(
        exchange(partial)
    )
    proj = exchange(copies)

    tables = [pltpu.SMEM(lengths.shape, jnp.int32), pltpu.SMEM(routes.shape, jnp.int32)]
    chips = groups // 2
    size, force, *send = call(
        states_kernel, "states",
        (struct((tokens, channels)),) * 2 + (struct((2, CAP, width, channels)),) * chips,
        [ANY, ANY] + [VMEM] * 5,
        out_specs=(VMEM,) * (2 + chips),
        scratch=tables
        + [
            f32(2 * width, tokens), f32(width, channels),
            f32(tokens, width, channels), f32(chips, 2, CAP, width, channels),
            pltpu.SemaphoreType.DMA((2,)),
        ],
    )(lengths, routes, proj, prefill_x, dt_weight, bias, a_log)

    def move(states, ahead, other):
        pairs = [
            (g, (g // 2 + (ahead if g % 2 == 0 else -ahead)) % chips * 2 + (g + other) % 2)
            for g in range(groups)
        ]
        return lax.ppermute(states, "group", pairs)

    arrived = [move(states, ahead, 0) for states, ahead in zip(send, far_first(chips)) if ahead]
    arrived.append(send[-1])
    prefill_out, mixed, unit, row_of = call(
        functools.partial(rest_kernel, groups=groups), "rest",
        (
            struct((tokens, channels), jnp.bfloat16), struct((total, channels)),
            struct((reach + 1, steps, width, channels)), struct((reach,), jnp.int32),
        ),
        [VMEM] * 7 + [ANY] * 6,
        out_specs=(VMEM, VMEM, VMEM, SMEM),
        scratch=tables[1:] + [
            bf16(tokens, channels), f32(1, channels), bf16(total, channels),
            bf16(total, channels), f32(rows, width, channels),
            pltpu.SMEM((reach,), jnp.int32),
            f32(total, channels), f32(total, channels), f32(total, channels),
            f32(total, channels), f32(channels // LANES, steps * 64, LANES),
            f32(2 * width, total), f32(width, channels), pltpu.SemaphoreType.DMA((6,)),
        ],
        flops=8 * 10**9,
    )(
        proj, dt_weight, a_log, bias, prefill_x, size, force, routes,
        *stay(prefill_gate, skip, decode_flat, gate_flat, cached_state),
    )
    swapped = move(
        call(
            pass_on_kernel, "pass_on", struct((chips, CAP, width, channels)),
            [ANY] + [VMEM] * chips,
        )(mixed, *arrived),
        0, 1,
    )
    decode_out = call(
        combine_kernel, "combine", struct((total, channels), jnp.bfloat16),
        [ANY] + [VMEM] * (3 + chips),
        scratch=[
            pltpu.SMEM((reach,), jnp.int32), f32(total, channels), pltpu.SemaphoreType.DMA((1,)),
        ],
    )(row_of, mixed, unit, swapped, *arrived)
    return prefill_out, decode_out.reshape(steps, rows, channels)


def solution(mesh):
    placed = (
        P("group", "tp"), P("group", "tp"), P("group", None), P(), P(None, "group", "tp"),
        P(None, "group", "tp"), P("group", None, "tp"), P("tp", None), P(None, "tp"), P("tp"),
        P(None, "tp"), P("tp"),
    )
    body = functools.partial(local, ranks=mesh.shape["tp"], groups=mesh.shape["group"])
    return jax.shard_map(
        body, mesh=mesh, in_specs=placed, out_specs=(P("group", "tp"), P(None, "group", "tp")),
        check_vma=False,
    )
```

```python
import functools

import jax
import jax.numpy as jnp
from jax import lax
from jax.experimental import pallas as pl
from jax.experimental.pallas import tpu as pltpu
from jax.sharding import PartitionSpec as P

LOG2E = 1.4426950408889634
FAR = 1e30
LANES = 128
CAP = 2

VMEM = pl.BlockSpec(memory_space=pltpu.VMEM)
SMEM = pl.BlockSpec(memory_space=pltpu.SMEM)
ANY = pl.BlockSpec(memory_space=pl.ANY)


def call(kernel, name, out_shape, in_specs, out_specs=VMEM, scratch=(), mib=16, flops=0):
    return pl.pallas_call(
        kernel,
        grid=(1,),
        out_shape=out_shape,
        in_specs=in_specs,
        out_specs=out_specs,
        scratch_shapes=scratch,
        compiler_params=pltpu.CompilerParams(vmem_limit_bytes=mib << 20),
        cost_estimate=pl.CostEstimate(flops=flops, bytes_accessed=1 << 20, transcendentals=0),
        name=name,
    )


def f32(*shape):
    return pltpu.VMEM(shape, jnp.float32)


def bf16(*shape):
    return pltpu.VMEM(shape, jnp.bfloat16)


def struct(shape, dtype=jnp.float32):
    return jax.ShapeDtypeStruct(shape, dtype)


def stay(*arrays):
    return tuple(pltpu.with_memory_space_constraint(a, pltpu.HBM) for a in arrays)


def fetch(sources, targets, sems):
    copies = [
        pltpu.make_async_copy(a, b, sems.at[i]) for i, (a, b) in enumerate(zip(sources, targets))
    ]
    for copy in copies:
        copy.start()
    return copies


def softplus(v):
    return jnp.maximum(v, 0.0) + jnp.log1p(jnp.exp(-jnp.abs(v)))


def silu(v):
    return v / (1.0 + jnp.exp(-v))


def tiles_of(channels):
    return [slice(t, t + LANES) for t in range(0, channels, LANES)]


def low_rows(rank, j, tile):
    first = j * (8 * (rank // LANES) + 2) + 8 * tile
    return slice(first, first + 8)


def vector_rows(rank, count, which):
    height = 8 * (rank // LANES) + 2
    return pl.ds(height - 2 + which, count, stride=height)


def low_part(proj_ref, rank, half, which):
    tiles = range(rank // LANES)
    return jnp.concatenate(
        [
            jnp.concatenate([proj_ref[low_rows(rank, j, tile), :] for tile in tiles], axis=1)
            for j in range(half * which, half * (which + 1))
        ],
        axis=0,
    )


def project_kernel(
    weight_hbm, prefill_hbm, decode_hbm, out_ref, weight_ref, prefill_ref, decode_ref, sems,
    *, rank,
):
    copies = fetch(
        (weight_hbm.at[: rank // 2], weight_hbm.at[rank // 2 :], prefill_hbm, decode_hbm),
        (weight_ref.at[: rank // 2], weight_ref.at[rank // 2 :], prefill_ref, decode_ref),
        sems,
    )
    count = weight_ref.shape[0] - rank
    for copy in copies:
        copy.wait()
    values = jnp.concatenate([prefill_ref[...], decode_ref[...]], axis=0)
    low = lax.dot_general(
        values, weight_ref[:rank], (((1,), (1,)), ((), ())), preferred_element_type=jnp.float32
    )
    for j in range(count):
        for tile, cols in enumerate(tiles_of(rank)):
            out_ref[low_rows(rank, j, tile), :] = low[8 * j : 8 * j + 8, cols]
    vectors = lax.dot_general(
        weight_ref[rank:], values, (((1,), (1,)), ((), ())), preferred_element_type=jnp.float32
    )
    rows = prefill_ref.shape[0]
    for which in range(2):
        out_ref[vector_rows(rank, count, which), :] = vectors[:, which * rows : (which + 1) * rows]


def total_kernel(parts_ref, out_ref, *, ranks):
    height = parts_ref.shape[0] // ranks
    group = 4
    quad = parts_ref[...].reshape(ranks // group, group * height, LANES).sum(axis=0)
    total = quad[:height]
    for i in range(1, group):
        total = total + quad[i * height : (i + 1) * height]
    quad = jnp.concatenate([total] * group, axis=0)
    for i in range(ranks // group):
        out_ref[i * group * height : (i + 1) * group * height, :] = quad


def step_sizes(low, weight_ref, bias_ref):
    low = low.astype(jnp.bfloat16)
    return softplus(
        jnp.dot(low, weight_ref[...], preferred_element_type=jnp.float32) + bias_ref[...]
    )


def fold(terms):
    return sum(terms[i : i + 8] for i in range(8, terms.shape[0], 8)) + terms[:8]


def gather_sums(part_ref, first, stride):
    return jnp.concatenate(
        [
            sum(
                (part_ref[tile, pl.ds(first + j, 8, stride=stride), :] for j in range(1, 8)),
                part_ref[tile, pl.ds(first, 8, stride=stride), :],
            )
            for tile in range(part_ref.shape[0])
        ],
        axis=1,
    )


def advance(hidden, rates_ref, size_row, forcing_row, inject, readout, part_ref, at):
    for tile, cols in enumerate(tiles_of(size_row.shape[1])):
        damping = jnp.exp2(size_row[:, cols] * rates_ref[:, cols])
        hidden[tile] = damping * hidden[tile] + forcing_row[:, cols] * inject
        if readout is not None:
            part_ref[tile, at : at + 8, :] = fold(readout * hidden[tile])


def prepare_scan(table, lengths_ref, proj_ref, x_ref, weight_ref, bias_ref, alog_ref, size_ref, force_ref, vec_ref, rates_ref):
    tokens, channels = x_ref.shape
    rank = weight_ref.shape[0]
    count = vec_ref.shape[0]
    low = low_part(proj_ref, rank, count // 2, 0)
    size = step_sizes(low, weight_ref, bias_ref)
    force_ref[...] = size * x_ref[...].astype(jnp.float32)
    vec_ref[...] = proj_ref[vector_rows(rank, count, 0), :]
    rates_ref[...] = -LOG2E * jnp.exp(alog_ref[...])
    table.wait()
    position = lax.broadcasted_iota(jnp.int32, (tokens, LANES), 0)
    first = position == 0
    begin = jnp.int32(0)
    ends = []
    for k in range(lengths_ref.shape[1]):
        first = first | (position == begin)
        begin = begin + lengths_ref[0, k]
        ends.append(begin - 1)
    reset = jnp.where(first, jnp.float32(FAR), jnp.float32(0.0))
    for cols in tiles_of(channels):
        size_ref[:, cols] = size[:, cols] + reset
    return ends


def scan(size_ref, force_ref, vec_ref, rates_ref, mixed_ref, part_ref, hist_ref):
    tokens, channels = size_ref.shape
    width = rates_ref.shape[0]
    tiles = tiles_of(channels)

    def block(b, hidden):
        base = pl.multiple_of(b * 8, 8)
        vectors = pltpu.roll(vec_ref[...], tokens - base, axis=1)
        sizes = size_ref[pl.ds(base, 8), :]
        forces = force_ref[pl.ds(base, 8), :]
        hidden = list(hidden)
        for i in range(8):
            inject = jnp.broadcast_to(vectors[:width, i : i + 1], (width, LANES))
            readout = None
            if mixed_ref is not None:
                readout = jnp.broadcast_to(vectors[width:, i : i + 1], (width, LANES))
            advance(
                hidden, rates_ref, sizes[i : i + 1], forces[i : i + 1], inject, readout,
                part_ref, i * 8,
            )
            if hist_ref is not None:
                for tile, cols in enumerate(tiles):
                    hist_ref[base + i, :, cols] = hidden[tile]
        if mixed_ref is not None:
            mixed_ref[pl.ds(base, 8), :] = gather_sums(part_ref, 0, 8)
        return tuple(hidden)

    zero = jnp.zeros((width, LANES), jnp.float32)
    lax.fori_loop(0, tokens // 8, block, (zero,) * len(tiles), unroll=16)


def places_on(source, dest, chips):
    on = dest // 2 - source // 2 + chips
    return lax.rem(jnp.where(lax.rem(source, 2) == 0, on, 2 * chips - on), chips)


def far_first(chips):
    return sorted(range(chips), key=lambda ahead: -min(ahead, chips - ahead))


def states_kernel(
    lengths_any, routes_any, proj_ref, x_ref, weight_ref, bias_ref, alog_ref,
    *rest,
):
    size_ref, force_ref, *send_refs = rest[:-7]
    lengths_ref, routes_ref, vec_ref, rates_ref, hist_ref, send_ref, sems = rest[-7:]
    tables = fetch((lengths_any, routes_any), (lengths_ref, routes_ref), sems)
    chips = len(send_refs)
    requests = lengths_ref.shape[1]
    group = lax.axis_index("group")
    ends = prepare_scan(
        tables[0], lengths_ref, proj_ref, x_ref, weight_ref, bias_ref, alog_ref, size_ref, force_ref, vec_ref,
        rates_ref,
    )
    scan(size_ref, force_ref, vec_ref, rates_ref, None, None, hist_ref)
    tables[1].wait()
    dests = [routes_ref[0, group * requests + k] for k in range(requests)]
    for k in range(requests):
        lane = jnp.int32(0)
        for j in range(k):
            lane = lane + (dests[j] == dests[k]).astype(jnp.int32)
        ahead = places_on(group, dests[k], chips)
        other = lax.rem(dests[k] + group, 2)
        send_ref[ahead, other, lane] = hist_ref[ends[k]]
    for ref, ahead in zip(send_refs, far_first(chips)):
        ref[...] = send_ref[ahead]


def rest_kernel(
    proj_ref, weight_ref, alog_ref, bias_ref, prefill_x_ref,
    prefill_size_ref, prefill_force_ref,
    routes_any, prefill_gate_hbm, skip_hbm, decode_x_hbm, decode_gate_hbm, state_hbm,
    out_ref, mixed_ref, unit_ref, row_ref,
    routes_ref, prefill_gate_ref, skip_ref, decode_x_ref, decode_gate_ref, state_ref,
    source_ref, size_ref, force_ref, act_ref, sum_ref, part_ref, vec_ref, rates_ref, sems, *, groups,
):
    copies = fetch(
        (routes_any, prefill_gate_hbm, skip_hbm, decode_x_hbm, decode_gate_hbm, state_hbm),
        (routes_ref, prefill_gate_ref, skip_ref, decode_x_ref, decode_gate_ref, state_ref),
        sems,
    )
    total, channels = decode_x_ref.shape
    rows, width = state_ref.shape[:2]
    steps = total // rows
    reach = source_ref.shape[0]
    tiles = tiles_of(channels)
    rank = weight_ref.shape[0]
    count = vec_ref.shape[0]
    requests = routes_ref.shape[1] // groups
    me = lax.axis_index("group")

    rates_ref[...] = -LOG2E * jnp.exp(alog_ref[...])
    vec_ref[...] = proj_ref[vector_rows(rank, count, 0), :]
    scan(prefill_size_ref, prefill_force_ref, vec_ref, rates_ref, sum_ref, part_ref, None)
    copies[1].wait()
    copies[2].wait()
    mixed = sum_ref[...] + skip_ref[...] * prefill_x_ref[...].astype(jnp.float32)
    out_ref[...] = (mixed * silu(prefill_gate_ref[...].astype(jnp.float32))).astype(out_ref.dtype)

    copies[0].wait()
    for n in range(reach):
        source_ref[n] = reach
        row_ref[n] = -1
    slot = jnp.int32(0)
    for g in range(groups):
        lane = jnp.int32(0)
        for k in range(requests):
            ours = routes_ref[0, g * requests + k] == me

            @pl.when(ours)
            def _(g=g, slot=slot, lane=lane):
                behind = places_on(jnp.int32(g), me, groups // 2)
                source = (behind * 2 + lax.rem(me + g, 2)) * CAP + lane
                source_ref[slot] = source
                row_ref[source] = slot

            slot = slot + ours.astype(jnp.int32)
            lane = lane + ours.astype(jnp.int32)

    copies[3].wait()
    copies[4].wait()
    size = step_sizes(low_part(proj_ref, rank, count // 2, 1), weight_ref, bias_ref)
    values = decode_x_ref[...].astype(jnp.float32)
    size_ref[...] = size
    force_ref[...] = size * values
    vec_ref[...] = proj_ref[vector_rows(rank, count, 1), :]
    act_ref[...] = silu(decode_gate_ref[...].astype(jnp.float32))
    copies[5].wait()

    def block(b, carry, units):
        base = pl.multiple_of(b * 8, 8)
        at = [pl.multiple_of(s * rows + base, 8) for s in range(steps)]
        vectors = [pltpu.roll(vec_ref[...], total - at[s], axis=1) for s in range(steps)]
        sizes = [size_ref[pl.ds(at[s], 8), :] for s in range(steps)]
        forces = [force_ref[pl.ds(at[s], 8), :] for s in range(steps)]
        acts = [act_ref[pl.ds(at[s], 8), :] for s in range(steps)]
        for i in range(8):
            hidden = [state_ref[base + i, :, cols] for cols in tiles]
            if units:
                source = source_ref[base + i]
                hidden = [jnp.where(source < reach, 0.0, start) for start in hidden]
            summed = None
            for s in range(steps):
                inject = jnp.broadcast_to(vectors[s][:width, i : i + 1], (width, LANES))
                readout = jnp.broadcast_to(vectors[s][width:, i : i + 1], (width, LANES))
                row = sizes[s][i : i + 1]
                advance(
                    hidden, rates_ref, row, forces[s][i : i + 1], inject, readout, part_ref,
                    (s * 8 + i) * 8,
                )
                if units:
                    summed = row if s == 0 else summed + row
                    for cols in tiles:
                        unit_ref[source, s, :, cols] = (
                            readout * acts[s][i : i + 1, cols]
                        ) * jnp.exp2(summed[:, cols] * rates_ref[:, cols])
        for s in range(steps):
            sum_ref[pl.ds(at[s], 8), :] = gather_sums(part_ref, s * 64, 8)
        return carry

    lax.fori_loop(0, reach // 8, functools.partial(block, units=True), 0)
    lax.fori_loop(reach // 8, rows // 8, functools.partial(block, units=False), 0)
    mixed_ref[...] = (sum_ref[...] + skip_ref[...] * values) * act_ref[...]


def pass_on_kernel(mixed_ref, *refs):
    for ref, ahead in zip(refs[:-1], far_first(len(refs) - 1)):
        refs[-1][ahead] = ref[1]


def combine_kernel(row_any, mixed_ref, unit_ref, swapped_ref, *rest):
    here_refs, (out_ref, row_ref, sum_ref, sems) = rest[:-4], rest[-4:]
    (table,) = fetch((row_any,), (row_ref,), sems)
    steps = unit_ref.shape[1]
    rows = mixed_ref.shape[0] // steps
    sum_ref[...] = mixed_ref[...]
    added = []
    for ref, ahead in zip(here_refs, far_first(len(here_refs))):
        for c in range(2 * CAP):
            state = ref[0, c] if c < CAP else swapped_ref[ahead, c - CAP]
            for s in range(steps):
                terms = unit_ref[2 * CAP * ahead + c, s] * state
                term = jnp.sum(terms, axis=0, keepdims=True)
                added.append((2 * CAP * ahead + c, s, term))
    table.wait()
    for slot, s, term in added:
        row = row_ref[slot]
        at = pl.ds(s * rows + jnp.maximum(row, 0), 1)
        sum_ref[at, :] = sum_ref[at, :] + jnp.where(row >= 0, term, 0.0)
    out_ref[...] = sum_ref[...].astype(out_ref.dtype)


def local(
    prefill_x, prefill_gate, lengths, routes, decode_x, decode_gate, cached_state, xproj_weight,
    dt_weight, dt_bias, a_log, skip_gain, *, ranks, groups,
):
    tokens, channels = prefill_x.shape
    steps, rows, _ = decode_x.shape
    width = a_log.shape[0]
    requests = lengths.shape[1]
    columns = xproj_weight.shape[1]
    total = steps * rows
    reach = groups * CAP
    decode_flat = decode_x.reshape(total, channels)
    gate_flat = decode_gate.reshape(total, channels)
    bias = dt_bias.reshape(1, channels)
    skip = skip_gain.reshape(1, channels)
    rank = dt_weight.shape[0]
    height = 8 * (rank // LANES) + 2
    routes = routes.T
    flat = struct((ranks * height, LANES))

    def exchange(rows):
        chunks = rows.reshape(ranks, height // 2, 2, LANES)
        return lax.all_to_all(chunks, "tp", 0, 0).reshape(ranks * height, LANES)

    partial = call(
        functools.partial(project_kernel, rank=rank), "project", flat, [ANY] * 3,
        scratch=[
            bf16(columns, channels), bf16(tokens, channels), bf16(total, channels),
            pltpu.SemaphoreType.DMA((4,)),
        ],
    )(*stay(xproj_weight.T, prefill_x, decode_flat))
    copies = call(functools.partial(total_kernel, ranks=ranks), "total", flat, [VMEM])(
        exchange(partial)
    )
    proj = exchange(copies)

    tables = [pltpu.SMEM(lengths.shape, jnp.int32), pltpu.SMEM(routes.shape, jnp.int32)]
    chips = groups // 2
    size, force, *send = call(
        states_kernel, "states",
        (struct((tokens, channels)),) * 2 + (struct((2, CAP, width, channels)),) * chips,
        [ANY, ANY] + [VMEM] * 5,
        out_specs=(VMEM,) * (2 + chips),
        scratch=tables
        + [
            f32(2 * width, tokens), f32(width, channels),
            f32(tokens, width, channels), f32(chips, 2, CAP, width, channels),
            pltpu.SemaphoreType.DMA((2,)),
        ],
    )(lengths, routes, proj, prefill_x, dt_weight, bias, a_log)

    def move(states, ahead, other):
        pairs = [
            (g, (g // 2 + (ahead if g % 2 == 0 else -ahead)) % chips * 2 + (g + other) % 2)
            for g in range(groups)
        ]
        return lax.ppermute(states, "group", pairs)

    arrived = [move(states, ahead, 0) for states, ahead in zip(send, far_first(chips)) if ahead]
    arrived.append(send[-1])
    prefill_out, mixed, unit, row_of = call(
        functools.partial(rest_kernel, groups=groups), "rest",
        (
            struct((tokens, channels), jnp.bfloat16), struct((total, channels)),
            struct((reach + 1, steps, width, channels)), struct((reach,), jnp.int32),
        ),
        [VMEM] * 7 + [ANY] * 6,
        out_specs=(VMEM, VMEM, VMEM, SMEM),
        scratch=tables[1:] + [
            bf16(tokens, channels), f32(1, channels), bf16(total, channels),
            bf16(total, channels), f32(rows, width, channels),
            pltpu.SMEM((reach,), jnp.int32),
            f32(total, channels), f32(total, channels), f32(total, channels),
            f32(total, channels), f32(channels // LANES, steps * 64, LANES),
            f32(2 * width, total), f32(width, channels), pltpu.SemaphoreType.DMA((6,)),
        ],
        flops=8 * 10**9,
    )(
        proj, dt_weight, a_log, bias, prefill_x, size, force, routes,
        *stay(prefill_gate, skip, decode_flat, gate_flat, cached_state),
    )
    swapped = move(
        call(
            pass_on_kernel, "pass_on", struct((chips, CAP, width, channels)),
            [ANY] + [VMEM] * chips,
        )(mixed, *arrived),
        0, 1,
    )
    decode_out = call(
        combine_kernel, "combine", struct((total, channels), jnp.bfloat16),
        [ANY] + [VMEM] * (3 + chips),
        scratch=[
            pltpu.SMEM((reach,), jnp.int32), f32(total, channels), pltpu.SemaphoreType.DMA((1,)),
        ],
    )(row_of, mixed, unit, swapped, *arrived)
    return prefill_out, decode_out.reshape(steps, rows, channels)


def solution(mesh):
    placed = (
        P("group", "tp"), P("group", "tp"), P("group", None), P(), P(None, "group", "tp"),
        P(None, "group", "tp"), P("group", None, "tp"), P("tp", None), P(None, "tp"), P("tp"),
        P(None, "tp"), P("tp"),
    )
    body = functools.partial(local, ranks=mesh.shape["tp"], groups=mesh.shape["group"])
    return jax.shard_map(
        body, mesh=mesh, in_specs=placed, out_specs=(P("group", "tp"), P(None, "group", "tp")),
        check_vma=False,
    )
```
